768 devices in a mesh: row: 8 (over y_hi, x), col: 96 (over z, y_lo, core).
Axes of the slice: x: 4, y: 8 (y_hi: 2, y_lo: 4; y = y_hi * 4 + y_lo), z: 12, core: 2. Of those that a mesh axis runs over, the one named last changes fastest.
Arguments:
- win_vals: bfloat16 [8, 96, 128, 128], P('row', 'col'), may hold values from -3 to 3
- couple_vals: bfloat16 [8, 96, 8, 12, 128, 128], P('row', 'col'), may hold values from -0.09375 to 0.09375
- win_cols: int32 [8, 96], replicated, may hold values from -1 to 862, as said below
Outputs:
- purified: bfloat16 [8, 96, 128, 128], P('row', 'col')
The draws below stay inside these ranges and needn't reach their ends.
Inputs may be any that keep to these rules, and one draw needn't show every extreme that they name: `win_cols`: slot s of window r is -1 (empty) or block column s * 9 + o with 0 <= o <= 7, so no window row is a live column; in one stripe the live columns of different windows differ. For every window and band b, the 12 slots s with s // 12 == b hold 1 to 8 live columns, and in some window every band holds exactly 8.
All inputs are finite; a program needn't handle non-finite values.
Results may differ from the reference program's by a relative error of at most 0.0035.
Values may be sent and summed in bfloat16 or wider, within the bound.
No kernel may reach another device: no remote copies, remote signals or barrier semaphores. Data moves between devices by JAX's collectives and lax.ppermute only.
A program may use at most 32 MiB of HBM per device.

```python
import jax
import jax.numpy as jnp
from jax import lax

BS = 128
TC = 9
G = 12
LIVE = 8
N_ROW = 8
N_COL = 96


def draw_win_cols(key, part):
    key = jax.random.fold_in(key, 7)
    count_key, order_key, offset_key, forced_key = jax.random.split(key, 4)
    counts = jax.random.randint(count_key, (N_ROW, N_ROW), 1, LIVE + 1).astype(jnp.int32)
    forced = jax.random.randint(forced_key, (), 0, N_ROW).astype(jnp.int32)
    windows = jnp.arange(N_ROW, dtype=jnp.int32)
    counts = jnp.where(windows[:, None] == forced, LIVE, counts)
    order_keys = jax.random.split(order_key, N_ROW * N_ROW)
    ranking = jax.vmap(lambda one_key: jax.random.permutation(one_key, G))(order_keys)
    ranking = ranking.reshape(N_ROW, N_ROW, G).astype(jnp.int32)
    alive_slots = (ranking < counts[:, :, None]).reshape(N_ROW, N_COL)
    offset_keys = jax.random.split(offset_key, N_COL)
    offsets = jax.vmap(lambda one_key: jax.random.permutation(one_key, TC - 1)[:N_ROW])(offset_keys).astype(jnp.int32)
    stripes = jnp.arange(N_COL, dtype=jnp.int32)
    columns = stripes[None, :] * TC + jnp.transpose(offsets)
    return jnp.where(alive_slots, columns, -1).astype(jnp.int32)


def steps_of(key, dims, pieces, least, largest):
    factor_of, own = 1.0, jax.random.fold_in(key, 6)
    for position, shards_of in pieces:
        draws = jnp.exp(jax.random.uniform(jax.random.fold_in(own, position), (shards_of,), jnp.float32, least / len(pieces), largest / len(pieces)))
        factor_of = factor_of * jnp.repeat(draws, dims[position] // shards_of).reshape([-1 if axis == position else 1 for axis in range(len(dims))])
    return factor_of


def bell_draw(own_key, extent, deviation, reach, cuts=(), kind=jnp.bfloat16):
    values = jax.random.normal(own_key, extent, jnp.float32) * deviation
    if len(cuts) > 0:
        values = steps_of(own_key, extent, cuts, -0.22, 0.18) * values
    return jnp.clip(values, min=-reach, max=reach).astype(kind)


def setup_inputs(seed: int = 0) -> dict:
    splits = jax.random.split(jax.random.key(seed), 4)
    win_vals = bell_draw(splits[0], (N_ROW, N_COL, BS, BS), 0.5, 3.0, ((0, 8), (1, 96)))
    couple_vals = bell_draw(splits[1], (N_ROW, N_COL, N_ROW, G, BS, BS), ((LIVE + 1) * N_ROW * BS // 2) ** -0.5, 0.09375, ((0, 8), (1, 96)))
    win_cols = draw_win_cols(jax.random.fold_in(splits[3], 71), 0)
    return dict(win_vals=win_vals, couple_vals=couple_vals, win_cols=win_cols)


def coupling_column(couple_vals, window_index, column_index):
    anchor = jnp.zeros((), jnp.int32)
    picked = lax.dynamic_slice(couple_vals, (anchor, column_index, window_index, anchor, anchor, anchor), (N_ROW, 1, 1, G, BS, BS))
    return picked.reshape(N_COL, BS, BS).astype(jnp.float32)


def reference(win_vals, couple_vals, win_cols):
    alive_all = win_cols >= 0
    column_ids = jnp.arange(N_COL, dtype=jnp.int32)

    def one_window(window_index):
        alive_mask = lax.dynamic_index_in_dim(alive_all, window_index, 0, keepdims=False)
        row_blocks = lax.dynamic_index_in_dim(win_vals, window_index, 0, keepdims=False).astype(jnp.float32)
        row_blocks = jnp.where(alive_mask[:, None, None], row_blocks, jnp.zeros_like(row_blocks))

        def times_coupling(source):
            def one_column(column_index):
                weights = coupling_column(couple_vals, window_index, column_index)
                return jnp.einsum("sab,sbc->ac", source, weights, precision=lax.Precision.HIGHEST)

            product = lax.map(one_column, column_ids)
            return jnp.where(alive_mask[:, None, None], product, jnp.zeros_like(product))

        square = times_coupling(row_blocks)
        square_half = lax.optimization_barrier(square.astype(jnp.bfloat16)).astype(jnp.float32)
        cube_blocks = times_coupling(square_half)
        return (3.0 * square - 2.0 * cube_blocks).astype(jnp.bfloat16)

    return lax.map(one_window, jnp.arange(N_ROW, dtype=jnp.int32))
```

```python
import functools

import jax
import jax.numpy as jnp
from jax import lax
from jax.experimental import pallas as pl
from jax.experimental.pallas import tpu as pltpu
from jax.sharding import PartitionSpec as P

BS = 128
BANDS = 8
GROUP = 12
LIVE = 8
Z, Y, C = 12, 4, 2
N_COL = Z * Y * C


def col_of(z, y, c):
    return (z * Y + y) * C + c


def member(cell, k):
    q, h = divmod(cell, Y // 2)
    return col_of(2 * q + (k >> 2 & 1), 2 * h + (k >> 1 & 1), k & 1)


CELLS = [[member(cell, k) for k in range(8)] for cell in range(12)]
SPREAD = [[member(cell, k) for cell in range(12)] for k in range(8)]
Y_LINES = [[col_of(z, y, c) for y in range(Y)] for z in range(Z) for c in range(C)]
Z_LINES = [[col_of(z, y, c) for z in range(Z)] for y in range(Y) for c in range(C)]
SWAP = [(s, s ^ 1) for s in range(N_COL)]
TO_SPREAD = [(GROUP * b + g, member(g, b)) for b in range(BANDS) for g in range(GROUP)]


def member_index(col):
    z = col // (Y * C)
    y = (col // C) % Y
    return (z % 2) * 4 + (y % 2) * 2 + col % C


def pack_kernel(cols_ref, couple_ref, out_ref):
    r = pl.program_id(0)
    first = lax.axis_index("row") * GROUP
    count = jnp.int32(0)
    for g in range(GROUP):
        alive = cols_ref[r, first + g] >= 0

        @pl.when(alive & (count < LIVE))
        def _(count=count, g=g):
            out_ref[0, count] = couple_ref[0, g]

        count = count + alive.astype(jnp.int32)
    for j in range(LIVE):

        @pl.when(j >= count)
        def _(j=j):
            out_ref[0, j] = jnp.zeros((BS, BS), out_ref.dtype)


def pack(win_cols, couple):
    return pl.pallas_call(
        pack_kernel,
        out_shape=jax.ShapeDtypeStruct((BANDS, LIVE, BS, BS), couple.dtype),
        grid=(BANDS,),
        in_specs=[
            pl.BlockSpec(memory_space=pltpu.SMEM),
            pl.BlockSpec((1, GROUP, BS, BS), lambda r: (r, 0, 0, 0)),
        ],
        out_specs=pl.BlockSpec((1, LIVE, BS, BS), lambda r: (r, 0, 0, 0)),
        cost_estimate=pl.CostEstimate(flops=0, bytes_accessed=5 << 20, transcendentals=0),
        name="pack",
    )(win_cols, couple)


def live_blocks(cols_ref, list_ref, r, band, position):
    count = jnp.int32(0)
    for g in range(GROUP):
        list_ref[jnp.minimum(count, LIVE)] = position(g)
        count = count + (cols_ref[r, band * GROUP + g] >= 0).astype(jnp.int32)
    return count


def picked(blocks_ref, list_ref, count):
    picks = []
    for j in range(LIVE):
        at = jnp.where(j < count, list_ref[j], 0)
        block = blocks_ref[at]
        picks.append(jnp.where(j < count, block, jnp.zeros_like(block)))
    return jnp.concatenate(picks, axis=1)


def square_kernel(cols_ref, a0_ref, a1_ref, b0_ref, b1_ref, m_ref, sq_ref, half_ref, xs, ms, lists, sems):
    row, col = lax.axis_index("row"), lax.axis_index("col")
    core = lax.rem(col, 2)
    part = Z * 2
    copies = [
        pltpu.make_async_copy(a0_ref, xs.at[core, pl.ds(0, part)], sems.at[0]),
        pltpu.make_async_copy(a1_ref, xs.at[core, pl.ds(part, part)], sems.at[1]),
        pltpu.make_async_copy(b0_ref, xs.at[1 - core, pl.ds(0, part)], sems.at[2]),
        pltpu.make_async_copy(b1_ref, xs.at[1 - core, pl.ds(part, part)], sems.at[3]),
        pltpu.make_async_copy(m_ref, ms, sems.at[4]),
    ]
    for copy in copies:
        copy.start()
    counts = []
    for band in range(BANDS):

        def position(g, band=band):
            z, rest = divmod(band * GROUP + g, Y * C)
            y, c = divmod(rest, C)
            return c * (2 * part) + (y // 2) * part + z * 2 + y % 2

        counts.append(live_blocks(cols_ref, lists.at[band], row, band, position))
    for copy in copies:
        copy.wait()
    blocks = xs.reshape(C * 2 * part, BS, BS)
    total = jnp.zeros((BS, BS), jnp.float32)
    for band in range(BANDS):
        left = picked(blocks, lists.at[band], counts[band])
        right = ms[band].reshape(LIVE * BS, BS)
        total = total + jnp.dot(left, right, preferred_element_type=jnp.float32)
    total = jnp.where(cols_ref[row, col] >= 0, total, 0.0)
    sq_ref[...] = total
    half_ref[...] = total.astype(half_ref.dtype)


def square_of(win_cols, xs, m):
    hbm = pl.BlockSpec(memory_space=pl.ANY)
    vmem = pl.BlockSpec(memory_space=pltpu.VMEM)
    return pl.pallas_call(
        square_kernel,
        out_shape=(
            jax.ShapeDtypeStruct((BS, BS), jnp.float32),
            jax.ShapeDtypeStruct((BS, BS), jnp.bfloat16),
        ),
        in_specs=[pl.BlockSpec(memory_space=pltpu.SMEM)] + [hbm] * 5,
        out_specs=(vmem, vmem),
        scratch_shapes=[
            pltpu.VMEM((C, 2 * Z * 2, BS, BS), jnp.bfloat16),
            pltpu.VMEM((BANDS, LIVE, BS, BS), jnp.bfloat16),
            pltpu.SMEM((BANDS, LIVE + 1), jnp.int32),
            pltpu.SemaphoreType.DMA((5,)),
        ],
        cost_estimate=pl.CostEstimate(flops=2 * 64 * BS**3, bytes_accessed=5 << 20, transcendentals=0),
        compiler_params=pltpu.CompilerParams(vmem_limit_bytes=24 << 20),
        name="square",
    )(win_cols, *xs, m)


def partial_kernel(cols_ref, x_ref, m_ref, out_ref, list_ref):
    row, col = lax.axis_index("row"), lax.axis_index("col")
    band = member_index(col)
    count = live_blocks(cols_ref, list_ref, row, band, lambda g: g)
    left = picked(x_ref, list_ref, count)
    for k in range(0, LIVE, 2):
        right = jnp.concatenate([m_ref[k].reshape(LIVE * BS, BS), m_ref[k + 1].reshape(LIVE * BS, BS)], axis=1)
        product = jnp.dot(left, right, preferred_element_type=jnp.float32)
        out_ref[k] = product[:, :BS].astype(out_ref.dtype)
        out_ref[k + 1] = product[:, BS:].astype(out_ref.dtype)


def partials_of(win_cols, x, m, dtype):
    vmem = pl.BlockSpec(memory_space=pltpu.VMEM)
    return pl.pallas_call(
        partial_kernel,
        out_shape=jax.ShapeDtypeStruct((8, BS, BS), dtype),
        in_specs=[pl.BlockSpec(memory_space=pltpu.SMEM), vmem, vmem],
        out_specs=vmem,
        scratch_shapes=[pltpu.SMEM((LIVE + 1,), jnp.int32)],
        cost_estimate=pl.CostEstimate(flops=2 * 64 * BS**3, bytes_accessed=3 << 20, transcendentals=0),
        compiler_params=pltpu.CompilerParams(vmem_limit_bytes=24 << 20),
        name="partials",
    )(win_cols, x, m)


def final_kernel(cols_ref, sq_ref, parts_ref, out_ref):
    row, col = lax.axis_index("row"), lax.axis_index("col")
    cube = parts_ref[0].astype(jnp.float32)
    for k in range(1, 8):
        cube = cube + parts_ref[k].astype(jnp.float32)
    value = 3.0 * sq_ref[...] - 2.0 * cube
    out_ref[...] = jnp.where(cols_ref[row, col] >= 0, value, 0.0).astype(out_ref.dtype)


def final_of(win_cols, sq, parts):
    vmem = pl.BlockSpec(memory_space=pltpu.VMEM)
    return pl.pallas_call(
        final_kernel,
        out_shape=jax.ShapeDtypeStruct((BS, BS), jnp.bfloat16),
        in_specs=[pl.BlockSpec(memory_space=pltpu.SMEM), vmem, vmem],
        out_specs=vmem,
        name="final",
    )(win_cols, sq, parts)


def exchange(value, axis, groups=None):
    return lax.all_to_all(value, axis, split_axis=0, concat_axis=0, tiled=True, axis_index_groups=groups)


def on_device(win_vals, couple_vals, win_cols):
    x = win_vals[0]
    packed = pack(win_cols, couple_vals[0, 0])
    column = exchange(packed, "row")

    line = exchange(jnp.broadcast_to(x, (Y, BS, BS)), "col", Y_LINES)
    own, other = [], []
    for half in (line[:2], line[2:]):
        gathered = lax.all_gather(half, "col", axis=0, tiled=True, axis_index_groups=Z_LINES)
        own.append(gathered)
        other.append(lax.ppermute(gathered, "col", SWAP))
    square, square_half = square_of(win_cols, own + other, column)

    cell = exchange(column, "col", CELLS)
    spread = lax.ppermute(square_half, "col", TO_SPREAD)
    blocks = exchange(jnp.broadcast_to(spread, (GROUP, BS, BS)), "col", SPREAD)
    parts = partials_of(win_cols, blocks, cell, jnp.float32)
    parts = exchange(parts, "col", CELLS)
    return final_of(win_cols, square, parts)[None, None]


def solution(mesh):
    return jax.shard_map(
        on_device,
        mesh=mesh,
        in_specs=(P("row", "col", None, None), P("row", "col", None, None, None, None), P()),
        out_specs=P("row", "col", None, None),
        check_vma=False,
    )
```

```python
import jax
import jax.numpy as jnp
from jax import lax
from jax.experimental import pallas as pl
from jax.experimental.pallas import tpu as pltpu
from jax.sharding import PartitionSpec as P

BS = 128
BANDS = 8
GROUP = 12
LIVE = 8
Z, Y, C = 12, 4, 2
N_COL = Z * Y * C


def col_of(z, y, c):
    return (z * Y + y) * C + c


def member(cell, k):
    q, h = divmod(cell, Y // 2)
    return col_of(2 * q + (k >> 2 & 1), 2 * h + (k >> 1 & 1), k & 1)


N_CELL = N_COL // 8
HALF = N_CELL // 2
CELLS = [[member(cell, k) for k in range(8)] for cell in range(N_CELL)]
HALVES = [[member(half * HALF + e, k) for e in range(HALF)] for half in range(2) for k in range(8)]


def device(row, col):
    return row * N_COL + col


def to_cells(shift, source):
    pairs = []
    for w in range(BANDS):
        for s in range(N_COL):
            b, g = divmod(s, GROUP)
            pairs.append((source(w, s), device(b, member((g + shift) % N_CELL, w))))
    return pairs


def home(w, s):
    return device(w, s)


CELL_OF = {member(cell, k): (cell, k) for cell in range(N_CELL) for k in range(8)}


def summed(w, s):
    cell, k = CELL_OF[s]
    return device(k, member(cell, w))


FROM_HOME = [to_cells(shift, home) for shift in (0, HALF)]
FROM_SUMMED = [to_cells(shift, summed) for shift in (0, HALF)]
TO_HOME = [(summed(w, s), home(w, s)) for w in range(BANDS) for s in range(N_COL)]


def cell_and_member(col):
    z = col // (Y * C)
    y = lax.rem(col // C, Y)
    cell = (z // 2) * (Y // 2) + y // 2
    return cell, lax.rem(z, 2) * 4 + lax.rem(y, 2) * 2 + lax.rem(col, 2)


def summed_slot(row, col):
    z = 2 * (col // (2 * Y * C)) + row // 4
    y = 2 * (lax.rem(col // C, Y) // 2) + lax.rem(row // 2, 2)
    return (z * Y + y) * C + lax.rem(row, 2)


def list_live(cols_ref, list_ref, window, band, position):
    count = jnp.int32(0)
    for g in range(GROUP):
        list_ref[jnp.minimum(count, LIVE)] = position(g)
        count = count + (cols_ref[window, band * GROUP + g] >= 0).astype(jnp.int32)
    return count


def pack_kernel(cols_ref, couple_ref, out_ref, lists, sem):
    band = lax.axis_index("row")
    for w in range(BANDS):
        count = list_live(cols_ref, lists.at[w], w, band, lambda g: g)
        for j in range(LIVE):
            at = jnp.where(j < count, lists[w, j], 0)
            pltpu.make_async_copy(couple_ref.at[w, at], out_ref.at[w, j], sem).start()
    pltpu.make_async_copy(out_ref, out_ref, sem).wait()


def pack(win_cols, couple):
    return pl.pallas_call(
        pack_kernel,
        out_shape=jax.ShapeDtypeStruct((BANDS, LIVE, BS, BS), couple.dtype),
        in_specs=[pl.BlockSpec(memory_space=pltpu.SMEM), pl.BlockSpec(memory_space=pl.ANY)],
        out_specs=pl.BlockSpec(memory_space=pl.ANY),
        scratch_shapes=[
            pltpu.SMEM((BANDS, LIVE + 1), jnp.int32),
            pltpu.SemaphoreType.DMA(()),
        ],
        cost_estimate=pl.CostEstimate(flops=0, bytes_accessed=4 << 20, transcendentals=0),
        compiler_params=pltpu.CompilerParams(vmem_limit_bytes=56 << 20),
        name="pack",
    )(win_cols, couple)


def partial_kernel(cols_ref, x_ref, m_ref, out_ref, list_ref):
    cell, window = cell_and_member(lax.axis_index("col"))
    second = cell // HALF

    def position(g):
        return (g % HALF) * 2 + (g // HALF != second).astype(jnp.int32)

    count = list_live(cols_ref, list_ref, window, lax.axis_index("row"), position)
    picks = []
    for j in range(LIVE):
        block = x_ref[jnp.where(j < count, list_ref[j], 0)]
        picks.append(jnp.where(j < count, block, jnp.zeros_like(block)))
    left = jnp.concatenate(picks, axis=1)
    for k in range(0, 8, 2):
        right = [m_ref[k + i].reshape(LIVE * BS, BS) for i in range(2)]
        product = jnp.dot(left, jnp.concatenate(right, axis=1), preferred_element_type=jnp.float32)
        for i in range(2):
            out_ref[k + i] = product[:, i * BS : (i + 1) * BS].astype(out_ref.dtype)


def partials_of(win_cols, x, m, dtype):
    vmem = pl.BlockSpec(memory_space=pltpu.VMEM)
    return pl.pallas_call(
        partial_kernel,
        out_shape=jax.ShapeDtypeStruct((8, BS, BS), dtype),
        in_specs=[pl.BlockSpec(memory_space=pltpu.SMEM), vmem, vmem],
        out_specs=vmem,
        scratch_shapes=[pltpu.SMEM((LIVE + 1,), jnp.int32)],
        cost_estimate=pl.CostEstimate(flops=2 * 64 * BS**3, bytes_accessed=3 << 20, transcendentals=0),
        compiler_params=pltpu.CompilerParams(vmem_limit_bytes=24 << 20),
        name="partials",
    )(win_cols, x, m)


def total_of(cols_ref, parts_ref):
    total = parts_ref[0].astype(jnp.float32)
    for b in range(1, BANDS):
        total = total + parts_ref[b].astype(jnp.float32)
    row, col = lax.axis_index("row"), lax.axis_index("col")
    _, window = cell_and_member(col)
    return total, cols_ref[window, summed_slot(row, col)] >= 0


def square_kernel(cols_ref, parts_ref, square_ref, half_ref):
    total, alive = total_of(cols_ref, parts_ref)
    total = jnp.where(alive, total, 0.0)
    square_ref[...] = total
    half_ref[...] = total.astype(half_ref.dtype)


def final_kernel(cols_ref, square_ref, parts_ref, out_ref):
    cube, alive = total_of(cols_ref, parts_ref)
    value = 3.0 * square_ref[...] - 2.0 * cube
    out_ref[...] = jnp.where(alive, value, 0.0).astype(out_ref.dtype)


def small_call(kernel, name, types, cols, *arrays):
    vmem = pl.BlockSpec(memory_space=pltpu.VMEM)
    return pl.pallas_call(
        kernel,
        out_shape=[jax.ShapeDtypeStruct((BS, BS), dtype) for dtype in types],
        in_specs=[pl.BlockSpec(memory_space=pltpu.SMEM)] + [vmem] * len(arrays),
        out_specs=[vmem] * len(types),
        name=name,
    )(cols, *arrays)


def exchange(value, axis, groups=None):
    return lax.all_to_all(value, axis, split_axis=0, concat_axis=0, tiled=True, axis_index_groups=groups)


def two_cells(block, routes):
    return jnp.stack([lax.ppermute(block, ("row", "col"), route) for route in routes])


def on_device(win_vals, couple_vals, win_cols):
    held = exchange(pack(win_cols, couple_vals[0, 0]), "col", CELLS)
    pair = two_cells(win_vals[0, 0], FROM_HOME)
    x = lax.all_gather(pair, "col", axis=0, tiled=True, axis_index_groups=HALVES)
    parts = exchange(partials_of(win_cols, x, held, jnp.float32), "row")
    square, square_half = small_call(square_kernel, "square", (jnp.float32, jnp.bfloat16), win_cols, parts)
    pair = two_cells(square_half, FROM_SUMMED)
    x = exchange(jnp.tile(pair, (HALF, 1, 1)), "col", HALVES)
    parts = exchange(partials_of(win_cols, x, held, jnp.float32), "row")
    (purified,) = small_call(final_kernel, "final", (jnp.bfloat16,), win_cols, square, parts)
    return lax.ppermute(purified, ("row", "col"), TO_HOME)[None, None]


def solution(mesh):
    return jax.shard_map(
        on_device,
        mesh=mesh,
        in_specs=(P("row", "col", None, None), P("row", "col", None, None, None, None), P()),
        out_specs=P("row", "col", None, None),
        check_vma=False,
    )
```

```python
import jax
import jax.numpy as jnp
from jax import lax
from jax.experimental import pallas as pl
from jax.experimental.pallas import tpu as pltpu
from jax.sharding import PartitionSpec as P

BS = 128
BANDS = 8
GROUP = 12
LIVE = 8
Z, Y, C = 12, 4, 2
N_COL = Z * Y * C


def col_of(z, y, c):
    return (z * Y + y) * C + c


def member(cell, k):
    q, h = divmod(cell, Y // 2)
    return col_of(2 * q + (k >> 2 & 1), 2 * h + (k >> 1 & 1), k & 1)


CELLS = [[member(cell, k) for k in range(8)] for cell in range(12)]
HALF = 6
HALVES = [[member(half * HALF + e, k) for e in range(HALF)] for half in range(2) for k in range(8)]
Y_NEAR = [[col_of(z, 2 * h + p, c) for p in range(2)] for z in range(Z) for h in range(2) for c in range(C)]
Y_FAR = [[col_of(z, 2 * h + p, c) for h in range(2)] for z in range(Z) for p in range(2) for c in range(C)]
Z_LINES = [[col_of(z, y, c) for z in range(Z)] for y in range(Y) for c in range(C)]
SWAP = [(s, s ^ 1) for s in range(N_COL)]
TO_CELLS = [
    [(GROUP * b + g, member((g + shift) % 12, b)) for b in range(BANDS) for g in range(GROUP)]
    for shift in (0, HALF)
]


def member_index(col):
    z = col // (Y * C)
    y = lax.rem(col // C, Y)
    return lax.rem(z, 2) * 4 + lax.rem(y, 2) * 2 + lax.rem(col, 2)


STEP = 4


def pack_kernel(cols_ref, couple_ref, out_ref, lists):
    band = lax.axis_index("row")
    for i in range(STEP):
        count = live_blocks(cols_ref, lists.at[i], pl.program_id(0) * STEP + i, band, lambda g: g)
        for j in range(LIVE):
            out_ref[i, j] = couple_ref[i, jnp.where(j < count, lists[i, j], 0)]


def pack(win_cols, couple):
    return pl.pallas_call(
        pack_kernel,
        out_shape=jax.ShapeDtypeStruct((BANDS, LIVE, BS, BS), couple.dtype),
        grid=(BANDS // STEP,),
        in_specs=[
            pl.BlockSpec(memory_space=pltpu.SMEM),
            pl.BlockSpec((STEP, GROUP, BS, BS), lambda i: (i, 0, 0, 0)),
        ],
        out_specs=pl.BlockSpec((STEP, LIVE, BS, BS), lambda i: (i, 0, 0, 0)),
        scratch_shapes=[pltpu.SMEM((STEP, LIVE + 1), jnp.int32)],
        cost_estimate=pl.CostEstimate(flops=0, bytes_accessed=5 << 20, transcendentals=0),
        compiler_params=pltpu.CompilerParams(vmem_limit_bytes=56 << 20),
        name="pack",
    )(win_cols, couple)


def live_blocks(cols_ref, list_ref, r, band, position):
    count = jnp.int32(0)
    for g in range(GROUP):
        list_ref[jnp.minimum(count, LIVE)] = position(g)
        count = count + (cols_ref[r, band * GROUP + g] >= 0).astype(jnp.int32)
    return count


def picked(blocks_ref, list_ref, count):
    picks = []
    for j in range(LIVE):
        at = jnp.where(j < count, list_ref[j], 0)
        block = blocks_ref[at]
        picks.append(jnp.where(j < count, block, jnp.zeros_like(block)))
    return jnp.concatenate(picks, axis=1)


def square_kernel(cols_ref, a0_ref, a1_ref, b0_ref, b1_ref, m_ref, sq_ref, half_ref, xs, lists, sems):
    row, col = lax.axis_index("row"), lax.axis_index("col")
    core = lax.rem(col, 2)
    part = Z * 2
    copies = [
        pltpu.make_async_copy(a0_ref, xs.at[core, pl.ds(0, part)], sems.at[0]),
        pltpu.make_async_copy(a1_ref, xs.at[core, pl.ds(part, part)], sems.at[1]),
        pltpu.make_async_copy(b0_ref, xs.at[1 - core, pl.ds(0, part)], sems.at[2]),
        pltpu.make_async_copy(b1_ref, xs.at[1 - core, pl.ds(part, part)], sems.at[3]),
    ]
    for copy in copies:
        copy.start()
    counts = []
    for band in range(BANDS):

        def position(g, band=band):
            z, rest = divmod(band * GROUP + g, Y * C)
            y, c = divmod(rest, C)
            return c * (2 * part) + (y // 2) * part + z * 2 + y % 2

        counts.append(live_blocks(cols_ref, lists.at[band], row, band, position))
    for copy in copies:
        copy.wait()
    blocks = xs.reshape(C * 2 * part, BS, BS)
    total = jnp.zeros((BS, BS), jnp.float32)
    for band in range(BANDS):
        left = picked(blocks, lists.at[band], counts[band])
        right = m_ref[band].reshape(LIVE * BS, BS)
        total = total + jnp.dot(left, right, preferred_element_type=jnp.float32)
    total = jnp.where(cols_ref[row, col] >= 0, total, 0.0)
    sq_ref[...] = total
    half_ref[...] = total.astype(half_ref.dtype)


def square_of(win_cols, xs, m):
    vmem = pl.BlockSpec(memory_space=pltpu.VMEM)
    return pl.pallas_call(
        square_kernel,
        out_shape=(
            jax.ShapeDtypeStruct((BS, BS), jnp.float32),
            jax.ShapeDtypeStruct((BS, BS), jnp.bfloat16),
        ),
        in_specs=[pl.BlockSpec(memory_space=pltpu.SMEM)] + [vmem] * 5,
        out_specs=(vmem, vmem),
        scratch_shapes=[
            pltpu.VMEM((C, 2 * Z * 2, BS, BS), jnp.bfloat16),
            pltpu.SMEM((BANDS, LIVE + 1), jnp.int32),
            pltpu.SemaphoreType.DMA((4,)),
        ],
        cost_estimate=pl.CostEstimate(flops=2 * 64 * BS**3, bytes_accessed=5 << 20, transcendentals=0),
        compiler_params=pltpu.CompilerParams(vmem_limit_bytes=24 << 20),
        name="square",
    )(win_cols, *xs, m)


def partial_kernel(cols_ref, x_ref, m_ref, out_ref, list_ref):
    row, col = lax.axis_index("row"), lax.axis_index("col")
    band = member_index(col)
    second = col // (N_COL // 2)

    def position(g):
        return (g % HALF) * 2 + (g // HALF != second).astype(jnp.int32)

    count = live_blocks(cols_ref, list_ref, row, band, position)
    left = picked(x_ref, list_ref, count)
    for k in range(0, LIVE, 2):
        right = jnp.concatenate([m_ref[k].reshape(LIVE * BS, BS), m_ref[k + 1].reshape(LIVE * BS, BS)], axis=1)
        product = jnp.dot(left, right, preferred_element_type=jnp.float32)
        out_ref[k] = product[:, :BS].astype(out_ref.dtype)
        out_ref[k + 1] = product[:, BS:].astype(out_ref.dtype)


def partials_of(win_cols, x, m, dtype):
    vmem = pl.BlockSpec(memory_space=pltpu.VMEM)
    return pl.pallas_call(
        partial_kernel,
        out_shape=jax.ShapeDtypeStruct((8, BS, BS), dtype),
        in_specs=[pl.BlockSpec(memory_space=pltpu.SMEM), vmem, vmem],
        out_specs=vmem,
        scratch_shapes=[pltpu.SMEM((LIVE + 1,), jnp.int32)],
        cost_estimate=pl.CostEstimate(flops=2 * 64 * BS**3, bytes_accessed=3 << 20, transcendentals=0),
        compiler_params=pltpu.CompilerParams(vmem_limit_bytes=24 << 20),
        name="partials",
    )(win_cols, x, m)


def final_kernel(cols_ref, sq_ref, parts_ref, out_ref):
    row, col = lax.axis_index("row"), lax.axis_index("col")
    cube = parts_ref[0].astype(jnp.float32)
    for k in range(1, 8):
        cube = cube + parts_ref[k].astype(jnp.float32)
    value = 3.0 * sq_ref[...] - 2.0 * cube
    out_ref[...] = jnp.where(cols_ref[row, col] >= 0, value, 0.0).astype(out_ref.dtype)


def final_of(win_cols, sq, parts):
    vmem = pl.BlockSpec(memory_space=pltpu.VMEM)
    return pl.pallas_call(
        final_kernel,
        out_shape=jax.ShapeDtypeStruct((BS, BS), jnp.bfloat16),
        in_specs=[pl.BlockSpec(memory_space=pltpu.SMEM), vmem, vmem],
        out_specs=vmem,
        name="final",
    )(win_cols, sq, parts)


def exchange(value, axis, groups=None):
    return lax.all_to_all(value, axis, split_axis=0, concat_axis=0, tiled=True, axis_index_groups=groups)


def on_device(win_vals, couple_vals, win_cols):
    packed = pack(win_cols, couple_vals[0, 0])
    column = exchange(packed, "row")

    gather = lambda value, groups: lax.all_gather(value, "col", axis=0, tiled=True, axis_index_groups=groups)
    x, packed = lax.optimization_barrier((win_vals[0], packed))
    line = gather(gather(x, Y_NEAR), Y_FAR)
    first = gather(line[:2], Z_LINES)
    first, late, column = lax.optimization_barrier((first, line[2:], column))
    own = [first, gather(late, Z_LINES)]
    other = [lax.ppermute(part, "col", SWAP) for part in own]
    square, square_half = square_of(win_cols, own + other, column)

    cell = exchange(column, "col", CELLS)
    pair = jnp.stack([lax.ppermute(square_half, "col", route) for route in TO_CELLS])
    pair, cell = lax.optimization_barrier((pair, cell))
    blocks = exchange(jnp.tile(pair, (HALF, 1, 1)), "col", HALVES)
    parts = partials_of(win_cols, blocks, cell, jnp.float32)
    parts = exchange(parts, "col", CELLS)
    return final_of(win_cols, square, parts)[None, None]


def solution(mesh):
    return jax.shard_map(
        on_device,
        mesh=mesh,
        in_specs=(P("row", "col", None, None), P("row", "col", None, None, None, None), P()),
        out_specs=P("row", "col", None, None),
        check_vma=False,
    )
```

```python
import jax
import jax.numpy as jnp
from jax import lax
from jax.experimental import pallas as pl
from jax.experimental.pallas import tpu as pltpu
from jax.sharding import PartitionSpec as P

BS = 128
BANDS = 8
GROUP = 12
Z, Y, C = 12, 4, 2
N_COL = Z * Y * C

QUAD = 4
CLASS = GROUP // QUAD


def col_of(z, y, c):
    return (z * Y + y) * C + c


Y_FAR = [[col_of(z, 2 * h + p, c) for h in range(2)] for z in range(Z) for p in range(2) for c in range(C)]
Y_NEAR = [[col_of(z, 2 * h + p, c) for p in range(2)] for z in range(Z) for h in range(2) for c in range(C)]
Z_LINES = [[col_of(z, y, c) for z in range(Z)] for y in range(Y) for c in range(C)]
CORES = [[s, s + 1] for s in range(0, N_COL, C)]
SPREAD = [[row * N_COL + quad + k for k in range(QUAD) for row in range(BANDS)] for quad in range(0, N_COL, QUAD)]


def partial_kernel(cols_ref, x_ref, m_ref, keep_ref, send_ref):
    row, col = lax.axis_index("row"), lax.axis_index("col")
    mine, core = lax.rem(col, QUAD), lax.rem(col, C)
    left = []
    for n in range(BANDS * CLASS):
        block = x_ref[n]
        left.append(jnp.where(cols_ref[row, n * QUAD + mine] >= 0, block, jnp.zeros_like(block)))
    left = jnp.concatenate(left, axis=1)
    for out_ref, which in ((keep_ref, core), (send_ref, 1 - core)):
        right = jnp.concatenate([m_ref[which], m_ref[2 + which]], axis=1)
        product = jnp.dot(left, right, preferred_element_type=jnp.float32)
        out_ref[0] = product[:, :BS]
        out_ref[1] = product[:, BS:]


def add_kernel(keep_ref, both_ref, keep_out, send_out):
    col = lax.axis_index("col")
    core, near = lax.rem(col, C), lax.rem(col // C, 2)
    other = (1 - core) * 2
    keep_out[...] = keep_ref[near] + both_ref[other + near]
    send_out[0] = keep_ref[1 - near] + both_ref[other + 1 - near]


def summed(cols_ref, keep_ref, both_ref):
    row, col = lax.axis_index("row"), lax.axis_index("col")
    near = lax.rem(col // C, 2)
    return keep_ref[...] + both_ref[1 - near], cols_ref[row, col] >= 0


def square_kernel(cols_ref, keep_ref, both_ref, square_ref, half_ref):
    total, alive = summed(cols_ref, keep_ref, both_ref)
    total = jnp.where(alive, total, 0.0)
    square_ref[...] = total
    half_ref[0] = total.astype(half_ref.dtype)


def final_kernel(cols_ref, keep_ref, both_ref, square_ref, out_ref):
    cube, alive = summed(cols_ref, keep_ref, both_ref)
    out_ref[...] = jnp.where(alive, 3.0 * square_ref[...] - 2.0 * cube, 0.0).astype(out_ref.dtype)


def call(kernel, name, outs, arrays, cols=None, **options):
    vmem = pl.BlockSpec(memory_space=pltpu.VMEM)
    scalars = () if cols is None else (cols,)
    return pl.pallas_call(
        kernel,
        out_shape=[jax.ShapeDtypeStruct(shape, dtype) for shape, dtype in outs],
        in_specs=[pl.BlockSpec(memory_space=pltpu.SMEM)] * len(scalars) + [vmem] * len(arrays),
        out_specs=[vmem] * len(outs),
        name=name,
        **options,
    )(*scalars, *arrays)


def gather(value, groups):
    return lax.all_gather(value, "col", axis=0, tiled=True, axis_index_groups=groups)


def product(win_cols, line, held):
    x = gather(line, Z_LINES)
    block, pair = (BS, BS), (2, BS, BS)
    keep, send = call(
        partial_kernel,
        "partials",
        [(pair, jnp.float32)] * 2,
        (x, held),
        win_cols,
        cost_estimate=pl.CostEstimate(flops=2 * 96 * BS**3, bytes_accessed=4 << 20, transcendentals=0),
        compiler_params=pltpu.CompilerParams(vmem_limit_bytes=24 << 20),
    )
    keep, send = call(add_kernel, "add", [(block, jnp.float32), ((1,) + block, jnp.float32)], (keep, gather(send, CORES)))
    return keep, gather(send, Y_NEAR)


def on_device(win_vals, couple_vals, win_cols):
    block = (BS, BS)
    classes = couple_vals[0, 0].reshape(BANDS, CLASS, QUAD, BS, BS).transpose(2, 0, 1, 3, 4)
    line = gather(win_vals[0], Y_FAR)
    line, classes = lax.optimization_barrier((line, classes.reshape(QUAD * BANDS, CLASS, BS, BS)))
    held = lax.all_to_all(classes, ("row", "col"), split_axis=0, concat_axis=0, tiled=True, axis_index_groups=SPREAD)
    held = held.reshape(QUAD, BANDS * CLASS * BS, BS)
    keep, both = product(win_cols, line, held)
    square, half = call(square_kernel, "square", [(block, jnp.float32), ((1,) + block, jnp.bfloat16)], (keep, both), win_cols)
    keep, both = product(win_cols, gather(half, Y_FAR), held)
    (purified,) = call(final_kernel, "final", [(block, jnp.bfloat16)], (keep, both, square), win_cols)
    return purified[None, None]


def solution(mesh):
    return jax.shard_map(
        on_device,
        mesh=mesh,
        in_specs=(P("row", "col", None, None), P("row", "col", None, None, None, None), P()),
        out_specs=P("row", "col", None, None),
        check_vma=False,
    )
```

```python
import jax
import jax.numpy as jnp
from jax import lax
from jax.experimental import pallas as pl
from jax.experimental.pallas import tpu as pltpu
from jax.sharding import PartitionSpec as P

BS = 128
BANDS = 8
GROUP = 12
LIVE = 8
Z, Y, C = 12, 4, 2
N_COL = Z * Y * C

QUAD = 4
CLASS = LIVE // QUAD
STEP = 4


def col_of(z, y, c):
    return (z * Y + y) * C + c


Y_FAR = [[col_of(z, 2 * h + p, c) for h in range(2)] for z in range(Z) for p in range(2) for c in range(C)]
Y_NEAR = [[col_of(z, 2 * h + p, c) for p in range(2)] for z in range(Z) for h in range(2) for c in range(C)]
Y_LINES = [[col_of(z, y, c) for y in range(Y)] for z in range(Z) for c in range(C)]
Z_LINES = [[col_of(z, y, c) for z in range(Z)] for y in range(Y) for c in range(C)]
CORES = [[s, s + 1] for s in range(0, N_COL, C)]
SPREAD = [[row * N_COL + quad + k for k in range(QUAD) for row in range(BANDS)] for quad in range(0, N_COL, QUAD)]


def list_live(cols_ref, list_ref, window, band, value):
    count = jnp.int32(0)
    for g in range(GROUP):
        list_ref[jnp.minimum(count, LIVE)] = value(g)
        count = count + (cols_ref[window, band * GROUP + g] >= 0).astype(jnp.int32)
    return count


def pack_kernel(cols_ref, couple_ref, out_ref, lists):
    band = lax.axis_index("row")
    for i in range(STEP):
        count = list_live(cols_ref, lists.at[i], pl.program_id(0) * STEP + i, band, lambda g: jnp.int32(g))
        for j in range(LIVE):
            out_ref[j % QUAD, i, j // QUAD] = couple_ref[i, jnp.where(j < count, lists[i, j], 0)]


def pack(win_cols, couple):
    return pl.pallas_call(
        pack_kernel,
        out_shape=jax.ShapeDtypeStruct((QUAD, BANDS, CLASS, BS, BS), couple.dtype),
        grid=(BANDS // STEP,),
        in_specs=[
            pl.BlockSpec(memory_space=pltpu.SMEM),
            pl.BlockSpec((STEP, GROUP, BS, BS), lambda i: (i, 0, 0, 0)),
        ],
        out_specs=pl.BlockSpec((QUAD, STEP, CLASS, BS, BS), lambda i: (0, i, 0, 0, 0)),
        scratch_shapes=[pltpu.SMEM((STEP, LIVE + 1), jnp.int32)],
        cost_estimate=pl.CostEstimate(flops=0, bytes_accessed=5 << 20, transcendentals=0),
        compiler_params=pltpu.CompilerParams(vmem_limit_bytes=56 << 20),
        name="pack",
    )(win_cols, couple)


def choose(cols_ref, quad, at):
    row, mine = lax.axis_index("row"), lax.rem(lax.axis_index("col"), QUAD)
    inside = lax.rem(quad, GROUP // QUAD)
    first = (quad - inside) * QUAD
    rank = jnp.int32(0)
    for g in range(GROUP - QUAD):
        alive = (cols_ref[row, first + g] >= 0) & (g < inside * QUAD)
        rank = rank + alive.astype(jnp.int32)
    found, place = jnp.int32(0), jnp.int32(0)
    for i in range(QUAD):
        alive = cols_ref[row, quad * QUAD + i] >= 0
        hit = alive & (lax.rem(rank, QUAD) == mine)
        place = jnp.where(hit, at(i), place)
        found = found + hit.astype(jnp.int32)
        rank = rank + alive.astype(jnp.int32)
    return place, found


def choose_plane_kernel(cols_ref, plane_ref, out_ref):
    z = lax.axis_index("col") // (Y * C)
    for h in range(2):
        place, found = choose(cols_ref, z * 2 + h, lambda i, h=h: (i % C) * Y + 2 * h + i // C)
        block = plane_ref[place]
        out_ref[h] = jnp.where(found > 0, block, jnp.zeros_like(block))


def choose_quad_kernel(cols_ref, quad_ref, out_ref):
    place, found = choose(cols_ref, lax.axis_index("col") // QUAD, lambda i: (i % C) * 2 + i // C)
    block = quad_ref[place]
    out_ref[0] = jnp.where(found > 0, block, jnp.zeros_like(block))


def partial_kernel(cols_ref, x_ref, m_ref, keep_ref, send_ref, list_ref):
    row, col = lax.axis_index("row"), lax.axis_index("col")
    mine, core = lax.rem(col, QUAD), lax.rem(col, C)
    left = []
    for band in range(BANDS):
        count = list_live(cols_ref, list_ref, row, band, lambda g, band=band: jnp.int32(band * 3 + g // QUAD))
        for i in range(CLASS):
            rank = mine + i * QUAD
            block = x_ref[jnp.where(rank < count, list_ref[rank], 0)]
            left.append(jnp.where(rank < count, block, jnp.zeros_like(block)))
    left = jnp.concatenate(left, axis=1)
    for out_ref, which in ((keep_ref, core), (send_ref, 1 - core)):
        right = jnp.concatenate([m_ref[which], m_ref[2 + which]], axis=1)
        product = jnp.dot(left, right, preferred_element_type=jnp.float32)
        out_ref[0] = product[:, :BS]
        out_ref[1] = product[:, BS:]


def add_both_kernel(keep_ref, both_ref, out_ref):
    other = (1 - lax.rem(lax.axis_index("col"), C)) * 2
    for p in range(2):
        out_ref[p] = keep_ref[p] + both_ref[other + p]


def add_kernel(keep_ref, both_ref, keep_out, send_out):
    col = lax.axis_index("col")
    core, near = lax.rem(col, C), lax.rem(col // C, 2)
    other = (1 - core) * 2
    keep_out[...] = keep_ref[near] + both_ref[other + near]
    send_out[0] = keep_ref[1 - near] + both_ref[other + 1 - near]


def square_kernel(cols_ref, both_ref, square_ref, half_ref):
    row, col = lax.axis_index("row"), lax.axis_index("col")
    core, near = lax.rem(col, C), lax.rem(col // C, 2)
    first = col // QUAD * QUAD + core
    for p in range(2):
        total = jnp.where(cols_ref[row, first + p * C] >= 0, both_ref[p] + both_ref[2 + p], 0.0)
        half_ref[p] = total.astype(half_ref.dtype)

        @pl.when(near == p)
        def _(total=total):
            square_ref[...] = total


def final_kernel(cols_ref, keep_ref, both_ref, square_ref, out_ref):
    row, col = lax.axis_index("row"), lax.axis_index("col")
    cube = keep_ref[...] + both_ref[1 - lax.rem(col // C, 2)]
    alive = cols_ref[row, col] >= 0
    out_ref[...] = jnp.where(alive, 3.0 * square_ref[...] - 2.0 * cube, 0.0).astype(out_ref.dtype)


def call(kernel, name, outs, arrays, cols=None, **options):
    vmem = pl.BlockSpec(memory_space=pltpu.VMEM)
    scalars = () if cols is None else (cols,)
    return pl.pallas_call(
        kernel,
        out_shape=[jax.ShapeDtypeStruct(shape, dtype) for shape, dtype in outs],
        in_specs=[pl.BlockSpec(memory_space=pltpu.SMEM)] * len(scalars) + [vmem] * len(arrays),
        out_specs=[vmem] * len(outs),
        name=name,
        **options,
    )(*scalars, *arrays)


def gather(value, groups):
    return lax.all_gather(value, "col", axis=0, tiled=True, axis_index_groups=groups)


def exchange(value, axis, groups):
    return lax.all_to_all(value, axis, split_axis=0, concat_axis=0, tiled=True, axis_index_groups=groups)


def product(win_cols, line, held):
    pair = ((2, BS, BS), jnp.float32)
    keep, send = call(
        partial_kernel,
        "partials",
        [pair] * 2,
        (gather(line, Z_LINES), held),
        win_cols,
        scratch_shapes=[pltpu.SMEM((LIVE + 1,), jnp.int32)],
        cost_estimate=pl.CostEstimate(flops=2 * 64 * BS**3, bytes_accessed=4 << 20, transcendentals=0),
        compiler_params=pltpu.CompilerParams(vmem_limit_bytes=24 << 20),
    )
    return keep, gather(send, CORES)


def on_device(win_vals, couple_vals, win_cols):
    block = (BS, BS)
    packed = pack(win_cols, couple_vals[0, 0])
    line = exchange(jnp.broadcast_to(win_vals[0], (Y,) + block), "col", Y_LINES)
    line, packed = lax.optimization_barrier((line, packed))
    held = exchange(packed.reshape((QUAD * BANDS, CLASS) + block), ("row", "col"), SPREAD)
    held = held.reshape(QUAD, BANDS * CLASS * BS, BS)
    chosen = [((2,) + block, jnp.bfloat16)]
    (line,) = call(choose_plane_kernel, "choose", chosen, (gather(line, CORES),), win_cols)

    keep, both = product(win_cols, line, held)
    (sums,) = call(add_both_kernel, "add", [((2,) + block, jnp.float32)], (keep, both))
    outs = [(block, jnp.float32), ((2,) + block, jnp.bfloat16)]
    square, half = call(square_kernel, "square", outs, (gather(sums, Y_NEAR),), win_cols)
    (chosen,) = call(choose_quad_kernel, "choose", [((1,) + block, jnp.bfloat16)], (gather(half, CORES),), win_cols)

    keep, both = product(win_cols, gather(chosen, Y_FAR), held)
    outs = [(block, jnp.float32), ((1,) + block, jnp.float32)]
    keep, send = call(add_kernel, "add", outs, (keep, both))
    (purified,) = call(final_kernel, "final", [(block, jnp.bfloat16)], (keep, gather(send, Y_NEAR), square), win_cols)
    return purified[None, None]


def solution(mesh):
    return jax.shard_map(
        on_device,
        mesh=mesh,
        in_specs=(P("row", "col", None, None), P("row", "col", None, None, None, None), P()),
        out_specs=P("row", "col", None, None),
        check_vma=False,
    )
```

```python
import jax
import jax.numpy as jnp
from jax import lax
from jax.experimental import pallas as pl
from jax.experimental.pallas import tpu as pltpu
from jax.sharding import PartitionSpec as P

BS = 128
BANDS = 8
GROUP = 12
LIVE = 8
Z, Y, C = 12, 4, 2
N_COL = Z * Y * C
QUADS = 2 * Z

CLASS = LIVE // 2
STEP = 4


def col_of(z, y, c):
    return (z * Y + y) * C + c


Y_LINES = [[col_of(z, y, c) for y in range(Y)] for z in range(Z) for c in range(C)]
Y_FAR = [[col_of(z, 2 * h + p, c) for h in range(2)] for z in range(Z) for p in range(2) for c in range(C)]
Y_NEAR = [[col_of(z, 2 * h + p, c) for p in range(2)] for z in range(Z) for h in range(2) for c in range(C)]
Z_LINES = [[col_of(z, y, c) for z in range(Z)] for y in range(Y) for c in range(C)]
SWAP = [(s, s ^ 1) for s in range(N_COL)]
SPREAD = [[row * N_COL + col for col in pair for row in range(BANDS)] for pair in Y_NEAR]


def place():
    col = lax.axis_index("col")
    return lax.axis_index("row"), col, lax.rem(col, C), lax.rem(col // C, 2)


def pair_alive(cols_ref, window, first):
    return [cols_ref[window, first + p * C] >= 0 for p in range(2)]


def member_of(alive, k):
    return jnp.where(alive[0] & alive[1], k, jnp.where(alive[0], 0, 1))


def list_live(cols_ref, list_ref, window, band, k, value):
    count, singles = jnp.int32(0), jnp.int32(0)
    for n in range(GROUP // 2):
        quad, core = divmod(n, C)
        alive = pair_alive(cols_ref, window, band * GROUP + quad * 4 + core)
        single = alive[0] != alive[1]
        taken = (alive[0] & alive[1]) | (single & (lax.rem(singles, 2) == k))
        list_ref[jnp.minimum(count, CLASS)] = value(quad, core, member_of(alive, k))
        count = count + taken.astype(jnp.int32)
        singles = singles + single.astype(jnp.int32)
    return count


def pack_kernel(cols_ref, couple_ref, out_ref, lists):
    band = lax.axis_index("row")
    for i in range(STEP):
        for k in range(2):
            slots = lists.at[i * 2 + k]
            count = list_live(
                cols_ref, slots, pl.program_id(0) * STEP + i, band, k, lambda quad, core, p: quad * 4 + p * C + core
            )
            for j in range(CLASS):
                out_ref[k, i, j] = couple_ref[i, jnp.where(j < count, slots[j], 0)]


def pack(win_cols, couple):
    return pl.pallas_call(
        pack_kernel,
        out_shape=jax.ShapeDtypeStruct((2, BANDS, CLASS, BS, BS), couple.dtype),
        grid=(BANDS // STEP,),
        in_specs=[
            pl.BlockSpec(memory_space=pltpu.SMEM),
            pl.BlockSpec((STEP, GROUP, BS, BS), lambda i: (i, 0, 0, 0)),
        ],
        out_specs=pl.BlockSpec((2, STEP, CLASS, BS, BS), lambda i: (0, i, 0, 0, 0)),
        scratch_shapes=[pltpu.SMEM((2 * STEP, CLASS + 1), jnp.int32)],
        cost_estimate=pl.CostEstimate(flops=0, bytes_accessed=5 << 20, transcendentals=0),
        compiler_params=pltpu.CompilerParams(vmem_limit_bytes=56 << 20),
        name="pack",
    )(win_cols, couple)


def choose_kernel(cols_ref, line_ref, out_ref):
    row, col, core, near = place()
    first = col // (Y * C) * (Y * C) + core
    for h in range(2):
        alive = pair_alive(cols_ref, row, first + 2 * h * C)
        out_ref[h] = line_ref[2 * h + member_of(alive, near)]


def partial_kernel(cols_ref, own_ref, other_ref, m_ref, *out_refs):
    *out_refs, list_ref = out_refs
    keep_ref, send_ref = out_refs if len(out_refs) == 2 else (out_refs[0].at[0], out_refs[0].at[1])
    row, _, core, near = place()
    left = []
    for band in range(BANDS):
        where = lambda quad, c, _, band=band: band * 3 + quad + jnp.where(core == c, 0, QUADS)
        count = list_live(cols_ref, list_ref, row, band, near, where)
        for j in range(CLASS):
            at = jnp.where(j < count, list_ref[j], 0)
            inside = lax.rem(at, QUADS)
            block = jnp.where(at < QUADS, own_ref[inside], other_ref[inside])
            left.append(jnp.where(j < count, block, jnp.zeros_like(block)))
    left = jnp.concatenate(left, axis=1)
    right = jnp.concatenate([m_ref[near], m_ref[1 - near]], axis=1)
    product = jnp.dot(left, right, preferred_element_type=jnp.float32)
    keep_ref[...] = product[:, :BS]
    send_ref[...] = product[:, BS:]


def square_kernel(cols_ref, sums_ref, square_ref, out_ref):
    row, col, core, near = place()
    alive = pair_alive(cols_ref, row, col - near * C)
    mine = sums_ref[near, 0] + sums_ref[1 - near, 1]
    theirs = sums_ref[near, 1] + sums_ref[1 - near, 0]
    is_alive = cols_ref[row, col] >= 0
    square_ref[...] = jnp.where(is_alive, mine, 0.0)
    out_ref[0] = jnp.where(member_of(alive, near) == near, mine, theirs).astype(out_ref.dtype)


def final_kernel(cols_ref, keep_ref, both_ref, square_ref, out_ref):
    row, col, _, near = place()
    cube = keep_ref[...] + both_ref[1 - near]
    alive = cols_ref[row, col] >= 0
    out_ref[...] = jnp.where(alive, 3.0 * square_ref[...] - 2.0 * cube, 0.0).astype(out_ref.dtype)


def call(kernel, name, outs, win_cols, *arrays, **options):
    vmem = pl.BlockSpec(memory_space=pltpu.VMEM)
    return pl.pallas_call(
        kernel,
        out_shape=[jax.ShapeDtypeStruct(shape, dtype) for shape, dtype in outs],
        in_specs=[pl.BlockSpec(memory_space=pltpu.SMEM)] + [vmem] * len(arrays),
        out_specs=[vmem] * len(outs),
        name=name,
        **options,
    )(win_cols, *arrays)


def gather(value, groups):
    return lax.all_gather(value, "col", axis=0, tiled=True, axis_index_groups=groups)


def exchange(value, axis, groups):
    return lax.all_to_all(value, axis, split_axis=0, concat_axis=0, tiled=True, axis_index_groups=groups)


def product(win_cols, line, held, shapes):
    own = gather(line, Z_LINES)
    other = lax.ppermute(own, "col", SWAP)
    return call(
        partial_kernel,
        "partials",
        [(shape, jnp.float32) for shape in shapes],
        win_cols,
        own,
        other,
        held,
        scratch_shapes=[pltpu.SMEM((CLASS + 1,), jnp.int32)],
        cost_estimate=pl.CostEstimate(flops=2 * 64 * BS**3, bytes_accessed=4 << 20, transcendentals=0),
        compiler_params=pltpu.CompilerParams(vmem_limit_bytes=24 << 20),
    )


def on_device(win_vals, couple_vals, win_cols):
    block = (BS, BS)
    packed = pack(win_cols, couple_vals[0, 0])
    line = exchange(jnp.broadcast_to(win_vals[0], (Y,) + block), "col", Y_LINES)
    line, packed = lax.optimization_barrier((line, packed))
    held = exchange(packed.reshape((2 * BANDS, CLASS) + block), ("row", "col"), SPREAD)
    held = held.reshape(2, BANDS * CLASS * BS, BS)
    (line,) = call(choose_kernel, "choose", [((2,) + block, jnp.bfloat16)], win_cols, line)

    (sums,) = product(win_cols, line, held, [(2,) + block])
    sums = gather(sums, Y_NEAR).reshape((2, 2) + block)
    outs = [(block, jnp.float32), ((1,) + block, jnp.bfloat16)]
    square, half = call(square_kernel, "square", outs, win_cols, sums)

    keep, send = product(win_cols, gather(half, Y_FAR), held, [block] * 2)
    both = gather(send[None], Y_NEAR)
    (purified,) = call(final_kernel, "final", [(block, jnp.bfloat16)], win_cols, keep, both, square)
    return purified[None, None]


def solution(mesh):
    return jax.shard_map(
        on_device,
        mesh=mesh,
        in_specs=(P("row", "col", None, None), P("row", "col", None, None, None, None), P()),
        out_specs=P("row", "col", None, None),
        check_vma=False,
    )
```

```python
import jax
import jax.numpy as jnp
from jax import lax
from jax.experimental import pallas as pl
from jax.experimental.pallas import tpu as pltpu
from jax.sharding import PartitionSpec as P

BS = 128
BANDS = 8
GROUP = 12
LIVE = 8
Z, Y, C = 12, 4, 2
N_COL = Z * Y * C
QUADS = 2 * Z

CLASS = LIVE // 2
STEP = 4


def col_of(z, y, c):
    return (z * Y + y) * C + c


Y_LINES = [[col_of(z, y, c) for y in range(Y)] for z in range(Z) for c in range(C)]
Y_FAR = [[col_of(z, 2 * h + p, c) for h in range(2)] for z in range(Z) for p in range(2) for c in range(C)]
Y_NEAR = [[col_of(z, 2 * h + p, c) for p in range(2)] for z in range(Z) for h in range(2) for c in range(C)]
Z_LINES = [[col_of(z, y, c) for z in range(Z)] for y in range(Y) for c in range(C)]
SWAP = [(s, s ^ 1) for s in range(N_COL)]
SPREAD = [[row * N_COL + col for col in pair for row in range(BANDS)] for pair in Y_NEAR]


def place():
    col = lax.axis_index("col")
    return lax.axis_index("row"), col, lax.rem(col, C), lax.rem(col // C, 2)


def pair_alive(cols_ref, window, first):
    return [cols_ref[window, first + p * C] >= 0 for p in range(2)]


def member_of(alive, k):
    return jnp.where(alive[0] & alive[1], k, jnp.where(alive[0], 0, 1))


def list_live(cols_ref, list_ref, window, band, k, value):
    count, singles = jnp.int32(0), jnp.int32(0)
    for n in range(GROUP // 2):
        quad, core = divmod(n, C)
        alive = pair_alive(cols_ref, window, band * GROUP + quad * 4 + core)
        single = alive[0] != alive[1]
        taken = (alive[0] & alive[1]) | (single & (lax.rem(singles, 2) == k))
        list_ref[jnp.minimum(count, CLASS)] = value(quad, core, member_of(alive, k))
        count = count + taken.astype(jnp.int32)
        singles = singles + single.astype(jnp.int32)
    return count


def pack_kernel(cols_ref, couple_ref, out_ref, lists):
    band = lax.axis_index("row")
    for i in range(STEP):
        for k in range(2):
            slots = lists.at[i * 2 + k]
            count = list_live(
                cols_ref, slots, pl.program_id(0) * STEP + i, band, k, lambda quad, core, p: quad * 4 + p * C + core
            )
            for j in range(CLASS):
                out_ref[k, i, j] = couple_ref[i, jnp.where(j < count, slots[j], 0)]


def pack(win_cols, couple):
    return pl.pallas_call(
        pack_kernel,
        out_shape=jax.ShapeDtypeStruct((2, BANDS, CLASS, BS, BS), couple.dtype),
        grid=(BANDS // STEP,),
        in_specs=[
            pl.BlockSpec(memory_space=pltpu.SMEM),
            pl.BlockSpec((STEP, GROUP, BS, BS), lambda i: (i, 0, 0, 0)),
        ],
        out_specs=pl.BlockSpec((2, STEP, CLASS, BS, BS), lambda i: (0, i, 0, 0, 0)),
        scratch_shapes=[pltpu.SMEM((2 * STEP, CLASS + 1), jnp.int32)],
        cost_estimate=pl.CostEstimate(flops=0, bytes_accessed=5 << 20, transcendentals=0),
        compiler_params=pltpu.CompilerParams(vmem_limit_bytes=56 << 20),
        name="pack",
    )(win_cols, couple)


def choose_kernel(cols_ref, line_ref, out_ref):
    row, col, core, near = place()
    first = col // (Y * C) * (Y * C) + core
    for h in range(2):
        alive = pair_alive(cols_ref, row, first + 2 * h * C)
        out_ref[h] = line_ref[2 * h + member_of(alive, near)]


def picked(cols_ref, own_ref, other_ref, list_ref):
    row, _, core, near = place()
    picks = []
    for band in range(BANDS):
        where = lambda quad, c, _, band=band: band * 3 + quad + jnp.where(core == c, 0, QUADS)
        count = list_live(cols_ref, list_ref, row, band, near, where)
        for j in range(CLASS):
            at = jnp.where(j < count, list_ref[j], 0)
            inside = lax.rem(at, QUADS)
            block = jnp.where(at < QUADS, own_ref[inside], other_ref[inside])
            picks.append(jnp.where(j < count, block, jnp.zeros_like(block)))
    return jnp.concatenate(picks, axis=1)


def multiply(cols_ref, left, m_ref, keep_ref, send_ref):
    row, col, _, near = place()
    alive = pair_alive(cols_ref, row, col - near * C)
    chosen = [m_ref[member_of(alive, k)] for k in (near, 1 - near)]
    product = jnp.dot(left, jnp.concatenate(chosen, axis=1), preferred_element_type=jnp.float32)
    keep_ref[...] = product[:, :BS]
    send_ref[...] = product[:, BS:]


def pick_kernel(cols_ref, own_ref, other_ref, left_ref, list_ref):
    left_ref[...] = picked(cols_ref, own_ref, other_ref, list_ref)


def multiply_kernel(cols_ref, left_ref, m_ref, keep_ref, send_ref):
    multiply(cols_ref, left_ref[...], m_ref, keep_ref, send_ref)


def partial_kernel(cols_ref, own_ref, other_ref, m_ref, keep_ref, send_ref, list_ref):
    multiply(cols_ref, picked(cols_ref, own_ref, other_ref, list_ref), m_ref, keep_ref, send_ref)


def square_kernel(keep_ref, both_ref, square_ref, half_ref):
    total = keep_ref[...] + both_ref[1 - place()[3]]
    square_ref[...] = total
    half_ref[0] = total.astype(half_ref.dtype)


def final_kernel(cols_ref, keep_ref, both_ref, square_ref, out_ref):
    row, col, _, near = place()
    cube = keep_ref[...] + both_ref[1 - near]
    alive = cols_ref[row, col] >= 0
    out_ref[...] = jnp.where(alive, 3.0 * square_ref[...] - 2.0 * cube, 0.0).astype(out_ref.dtype)


def call(kernel, name, outs, arrays, scalars=(), grant=4, **options):
    vmem = pl.BlockSpec(memory_space=pltpu.VMEM)
    return pl.pallas_call(
        kernel,
        out_shape=[jax.ShapeDtypeStruct(shape, dtype) for shape, dtype in outs],
        in_specs=[pl.BlockSpec(memory_space=pltpu.SMEM)] * len(scalars) + [vmem] * len(arrays),
        out_specs=[vmem] * len(outs),
        compiler_params=pltpu.CompilerParams(vmem_limit_bytes=grant << 20),
        name=name,
        **options,
    )(*scalars, *arrays)


def gather(value, groups):
    return lax.all_gather(value, "col", axis=0, tiled=True, axis_index_groups=groups)


def exchange(value, axis, groups):
    return lax.all_to_all(value, axis, split_axis=0, concat_axis=0, tiled=True, axis_index_groups=groups)


def lines(line):
    own = gather(line, Z_LINES)
    return own, lax.ppermute(own, "col", SWAP)


def on_device(win_vals, couple_vals, win_cols):
    block, cols = (BS, BS), (win_cols,)
    lists = dict(scratch_shapes=[pltpu.SMEM((CLASS + 1,), jnp.int32)])
    flops = lambda count: pl.CostEstimate(flops=count * BS**3, bytes_accessed=4 << 20, transcendentals=0)
    shares = [(block, jnp.float32)] * 2

    packed = pack(win_cols, couple_vals[0, 0])
    line = exchange(jnp.broadcast_to(win_vals[0], (Y,) + block), "col", Y_LINES)
    line, packed = lax.optimization_barrier((line, packed))
    held = exchange(packed.reshape((2 * BANDS, CLASS) + block), ("row", "col"), SPREAD)
    held = held.reshape(2, BANDS * CLASS * BS, BS)
    (line,) = call(choose_kernel, "choose", [((2,) + block, jnp.bfloat16)], (line,), cols)
    left = [((BS, BANDS * CLASS * BS), jnp.bfloat16)]
    (left,) = call(pick_kernel, "pick", left, lines(line), cols, 8, **lists)
    keep, send = call(multiply_kernel, "multiply", shares, (left, held), cols, 16, cost_estimate=flops(128))

    outs = [(block, jnp.float32), ((1,) + block, jnp.bfloat16)]
    square, half = call(square_kernel, "square", outs, (keep, gather(send[None], Y_NEAR)))

    line = lines(gather(half, Y_FAR))
    keep, send = call(partial_kernel, "partials", shares, (*line, held), cols, 16, cost_estimate=flops(128), **lists)
    outs = [(block, jnp.bfloat16)]
    (purified,) = call(final_kernel, "final", outs, (keep, gather(send[None], Y_NEAR), square), cols)
    return purified[None, None]


def solution(mesh):
    return jax.shard_map(
        on_device,
        mesh=mesh,
        in_specs=(P("row", "col", None, None), P("row", "col", None, None, None, None), P()),
        out_specs=P("row", "col", None, None),
        check_vma=False,
    )
```

```python
import jax
import jax.numpy as jnp
from jax import lax
from jax.experimental import pallas as pl
from jax.experimental.pallas import tpu as pltpu
from jax.sharding import PartitionSpec as P

BS = 128
BANDS = 8
GROUP = 12
LIVE = 8
Z, Y, C = 12, 4, 2
N_COL = Z * Y * C
QUADS = 2 * Z

CLASS = LIVE // 2
STEP = 4


def col_of(z, y, c):
    return (z * Y + y) * C + c


Y_LINES = [[col_of(z, y, c) for y in range(Y)] for z in range(Z) for c in range(C)]
Y_NEAR = [[col_of(z, 2 * h + p, c) for p in range(2)] for z in range(Z) for h in range(2) for c in range(C)]
Z_LINES = [[col_of(z, y, c) for z in range(Z)] for y in range(Y) for c in range(C)]
SWAP = [(s, s ^ 1) for s in range(N_COL)]
SPREAD = [[row * N_COL + col for col in pair for row in range(BANDS)] for pair in Y_NEAR]


def place():
    col = lax.axis_index("col")
    return lax.axis_index("row"), col, lax.rem(col, C), lax.rem(col // C, 2)


def pair_alive(cols_ref, window, first):
    return [cols_ref[window, first + p * C] >= 0 for p in range(2)]


def member_of(alive, k):
    return jnp.where(alive[0] & alive[1], k, jnp.where(alive[0], 0, 1))


def list_live(cols_ref, list_ref, window, band, k, value):
    count, singles = jnp.int32(0), jnp.int32(0)
    for n in range(GROUP // 2):
        quad, core = divmod(n, C)
        alive = pair_alive(cols_ref, window, band * GROUP + quad * 4 + core)
        single = alive[0] != alive[1]
        taken = (alive[0] & alive[1]) | (single & (lax.rem(singles, 2) == k))
        list_ref[jnp.minimum(count, CLASS)] = value(quad, core, member_of(alive, k))
        count = count + taken.astype(jnp.int32)
        singles = singles + single.astype(jnp.int32)
    return count


def pack_kernel(cols_ref, couple_ref, out_ref, lists):
    band = lax.axis_index("row")
    for i in range(STEP):
        for k in range(2):
            slots = lists.at[i * 2 + k]
            count = list_live(
                cols_ref, slots, pl.program_id(0) * STEP + i, band, k, lambda quad, core, p: quad * 4 + p * C + core
            )
            for j in range(CLASS):
                out_ref[k, i, j] = couple_ref[i, jnp.where(j < count, slots[j], 0)]


def pack(win_cols, couple):
    return pl.pallas_call(
        pack_kernel,
        out_shape=jax.ShapeDtypeStruct((2, BANDS, CLASS, BS, BS), couple.dtype),
        grid=(BANDS // STEP,),
        in_specs=[
            pl.BlockSpec(memory_space=pltpu.SMEM),
            pl.BlockSpec((STEP, GROUP, BS, BS), lambda i: (i, 0, 0, 0)),
        ],
        out_specs=pl.BlockSpec((2, STEP, CLASS, BS, BS), lambda i: (0, i, 0, 0, 0)),
        scratch_shapes=[pltpu.SMEM((2 * STEP, CLASS + 1), jnp.int32)],
        cost_estimate=pl.CostEstimate(flops=0, bytes_accessed=5 << 20, transcendentals=0),
        compiler_params=pltpu.CompilerParams(vmem_limit_bytes=56 << 20),
        name="pack",
    )(win_cols, couple)


def copies_kernel(x_ref, out_ref):
    for y in range(Y):
        out_ref[y] = x_ref[0]


def choose_kernel(cols_ref, line_ref, out_ref):
    row, col, core, near = place()
    first = col // (Y * C) * (Y * C) + core
    for h in range(2):
        alive = pair_alive(cols_ref, row, first + 2 * h * C)
        out_ref[h] = line_ref[2 * h + member_of(alive, near)]


def picked(cols_ref, own_ref, other_ref, list_ref):
    row, _, core, near = place()
    picks = []
    for band in range(BANDS):
        where = lambda quad, c, _, band=band: band * 3 + quad + jnp.where(core == c, 0, QUADS)
        count = list_live(cols_ref, list_ref, row, band, near, where)
        for j in range(CLASS):
            at = jnp.where(j < count, list_ref[j], 0)
            inside = lax.rem(at, QUADS)
            block = jnp.where(at < QUADS, own_ref[inside], other_ref[inside])
            picks.append(jnp.where(j < count, block, jnp.zeros_like(block)))
    return jnp.concatenate(picks, axis=1)


def multiply(cols_ref, left, m_ref):
    row, col, _, near = place()
    alive = pair_alive(cols_ref, row, col - near * C)
    chosen = [m_ref[member_of(alive, k)] for k in range(2)]
    product = jnp.dot(left, jnp.concatenate(chosen, axis=1), preferred_element_type=jnp.float32)
    return product[:, :BS], product[:, BS:]


def pick_kernel(cols_ref, own_ref, other_ref, left_ref, list_ref):
    left_ref[...] = picked(cols_ref, own_ref, other_ref, list_ref)


def multiply_kernel(cols_ref, left_ref, m_ref, out_ref):
    shares = multiply(cols_ref, left_ref[...], m_ref)
    for y in range(Y):
        out_ref[y] = shares[y % 2]


def partial_kernel(cols_ref, own_ref, other_ref, m_ref, keep_ref, send_ref, list_ref):
    shares = multiply(cols_ref, picked(cols_ref, own_ref, other_ref, list_ref), m_ref)
    near = place()[3]
    keep_ref[...] = jnp.where(near == 0, *shares)
    send_ref[...] = jnp.where(near == 0, *shares[::-1])


def square_kernel(shares_ref, square_ref, half_ref):
    h = lax.rem(lax.axis_index("col") // (2 * C), 2)
    square_ref[...] = shares_ref[2 * h] + shares_ref[2 * h + 1]
    for pair in range(2):
        half_ref[pair] = (shares_ref[2 * pair] + shares_ref[2 * pair + 1]).astype(half_ref.dtype)


def final_kernel(cols_ref, keep_ref, both_ref, square_ref, out_ref):
    row, col, _, near = place()
    cube = keep_ref[...] + both_ref[1 - near]
    alive = cols_ref[row, col] >= 0
    out_ref[...] = jnp.where(alive, 3.0 * square_ref[...] - 2.0 * cube, 0.0).astype(out_ref.dtype)


def call(kernel, name, outs, arrays, scalars=(), grant=4, **options):
    vmem = pl.BlockSpec(memory_space=pltpu.VMEM)
    return pl.pallas_call(
        kernel,
        out_shape=[jax.ShapeDtypeStruct(shape, dtype) for shape, dtype in outs],
        in_specs=[pl.BlockSpec(memory_space=pltpu.SMEM)] * len(scalars) + [vmem] * len(arrays),
        out_specs=[vmem] * len(outs),
        compiler_params=pltpu.CompilerParams(vmem_limit_bytes=grant << 20),
        name=name,
        **options,
    )(*scalars, *arrays)


def gather(value, groups):
    return lax.all_gather(value, "col", axis=0, tiled=True, axis_index_groups=groups)


def exchange(value, axis, groups):
    return lax.all_to_all(value, axis, split_axis=0, concat_axis=0, tiled=True, axis_index_groups=groups)


def lines(line):
    own = gather(line, Z_LINES)
    return own, lax.ppermute(own, "col", SWAP)


def on_device(win_vals, couple_vals, win_cols):
    block, cols = (BS, BS), (win_cols,)
    lists = dict(scratch_shapes=[pltpu.SMEM((CLASS + 1,), jnp.int32)])
    flops = lambda count: pl.CostEstimate(flops=count * BS**3, bytes_accessed=4 << 20, transcendentals=0)
    shares = [(block, jnp.float32)] * 2

    packed = pack(win_cols, couple_vals[0, 0])
    (line,) = call(copies_kernel, "copies", [((Y,) + block, jnp.bfloat16)], (win_vals[0],))
    line = exchange(line, "col", Y_LINES)
    line, packed = lax.optimization_barrier((line, packed))
    held = exchange(packed.reshape((2 * BANDS, CLASS) + block), ("row", "col"), SPREAD)
    held = held.reshape(2, BANDS * CLASS * BS, BS)
    (line,) = call(choose_kernel, "choose", [((2,) + block, jnp.bfloat16)], (line,), cols)
    left = [((BS, BANDS * CLASS * BS), jnp.bfloat16)]
    (left,) = call(pick_kernel, "pick", left, lines(line), cols, 8, **lists)
    outs = [((Y,) + block, jnp.float32)]
    (sums,) = call(multiply_kernel, "multiply", outs, (left, held), cols, 16, cost_estimate=flops(128))

    outs = [(block, jnp.float32), ((2,) + block, jnp.bfloat16)]
    square, half = call(square_kernel, "square", outs, (exchange(sums, "col", Y_LINES),))

    line = lines(half)
    keep, send = call(partial_kernel, "partials", shares, (*line, held), cols, 16, cost_estimate=flops(128), **lists)
    outs = [(block, jnp.bfloat16)]
    (purified,) = call(final_kernel, "final", outs, (keep, gather(send[None], Y_NEAR), square), cols)
    return purified[None, None]


def solution(mesh):
    return jax.shard_map(
        on_device,
        mesh=mesh,
        in_specs=(P("row", "col", None, None), P("row", "col", None, None, None, None), P()),
        out_specs=P("row", "col", None, None),
        check_vma=False,
    )
```

```python
import jax
import jax.numpy as jnp
from jax import lax
from jax.experimental import pallas as pl
from jax.experimental.pallas import tpu as pltpu
from jax.sharding import PartitionSpec as P

BS = 128
BANDS = 8
GROUP = 12
LIVE = 8
Z, Y, C = 12, 4, 2
N_COL = Z * Y * C
QUADS = 2 * Z

CLASS = LIVE // 2
STEP = 4


def col_of(z, y, c):
    return (z * Y + y) * C + c


Y_LINES = [[col_of(z, y, c) for y in range(Y)] for z in range(Z) for c in range(C)]
Y_NEAR = [[col_of(z, 2 * h + p, c) for p in range(2)] for z in range(Z) for h in range(2) for c in range(C)]
Z_LINES = [[col_of(z, y, (z + c) % C) for z in range(Z)] for y in range(Y) for c in range(C)]
SWAP = [(s, s ^ 1) for s in range(N_COL)]
SPREAD = [[row * N_COL + col for col in pair for row in range(BANDS)] for pair in Y_NEAR]


def place():
    col = lax.axis_index("col")
    return lax.axis_index("row"), col, lax.rem(col, C), lax.rem(col // C, 2)


def pair_alive(cols_ref, window, first):
    return [cols_ref[window, first + p * C] >= 0 for p in range(2)]


def member_of(alive, k):
    return jnp.where(alive[0] & alive[1], k, jnp.where(alive[0], 0, 1))


def list_live(cols_ref, list_ref, window, band, k, value):
    count, singles = jnp.int32(0), jnp.int32(0)
    for n in range(GROUP // 2):
        quad, core = divmod(n, C)
        alive = pair_alive(cols_ref, window, band * GROUP + quad * 4 + core)
        single = alive[0] != alive[1]
        taken = (alive[0] & alive[1]) | (single & (lax.rem(singles, 2) == k))
        list_ref[jnp.minimum(count, CLASS)] = value(quad, core, member_of(alive, k))
        count = count + taken.astype(jnp.int32)
        singles = singles + single.astype(jnp.int32)
    return count


def pack_kernel(cols_ref, couple_ref, out_ref, lists):
    band = lax.axis_index("row")
    for i in range(STEP):
        for k in range(2):
            slots = lists.at[i * 2 + k]
            count = list_live(
                cols_ref, slots, pl.program_id(0) * STEP + i, band, k, lambda quad, core, p: quad * 4 + p * C + core
            )
            for j in range(CLASS):
                out_ref[k, i, j] = couple_ref[i, jnp.where(j < count, slots[j], 0)]


def pack(win_cols, couple):
    return pl.pallas_call(
        pack_kernel,
        out_shape=jax.ShapeDtypeStruct((2, BANDS, CLASS, BS, BS), couple.dtype),
        grid=(BANDS // STEP,),
        in_specs=[
            pl.BlockSpec(memory_space=pltpu.SMEM),
            pl.BlockSpec((STEP, GROUP, BS, BS), lambda i: (i, 0, 0, 0)),
        ],
        out_specs=pl.BlockSpec((2, STEP, CLASS, BS, BS), lambda i: (0, i, 0, 0, 0)),
        scratch_shapes=[pltpu.SMEM((2 * STEP, CLASS + 1), jnp.int32)],
        cost_estimate=pl.CostEstimate(flops=0, bytes_accessed=5 << 20, transcendentals=0),
        compiler_params=pltpu.CompilerParams(vmem_limit_bytes=56 << 20),
        name="pack",
    )(win_cols, couple)


def copies_kernel(x_ref, out_ref):
    for y in range(Y):
        out_ref[y] = x_ref[0]


def choose_kernel(cols_ref, line_ref, out_ref):
    row, col, core, near = place()
    first = col // (Y * C) * (Y * C) + core
    for h in range(2):
        alive = pair_alive(cols_ref, row, first + 2 * h * C)
        out_ref[h] = line_ref[2 * h + member_of(alive, near)]


def picked(cols_ref, own_ref, other_ref, list_ref):
    row, col, core, near = place()
    line = lax.rem(col // (Y * C) + core, 2)
    picks = []
    for band in range(BANDS):
        where = lambda quad, c, _, band=band: (
            band * 3 + quad + QUADS * lax.rem(line + c + (band * 3 + quad) // 2, 2)
        )
        count = list_live(cols_ref, list_ref, row, band, near, where)
        for j in range(CLASS):
            at = jnp.where(j < count, list_ref[j], 0)
            inside = lax.rem(at, QUADS)
            block = jnp.where(at < QUADS, own_ref[inside], other_ref[inside])
            picks.append(jnp.where(j < count, block, jnp.zeros_like(block)))
    return jnp.concatenate(picks, axis=1)


def multiply(cols_ref, left, m_ref):
    row, col, _, near = place()
    alive = pair_alive(cols_ref, row, col - near * C)
    chosen = [m_ref[member_of(alive, k)] for k in range(2)]
    product = jnp.dot(left, jnp.concatenate(chosen, axis=1), preferred_element_type=jnp.float32)
    return product[:, :BS], product[:, BS:]


def pick_kernel(cols_ref, own_ref, other_ref, left_ref, list_ref):
    left_ref[...] = picked(cols_ref, own_ref, other_ref, list_ref)


def multiply_kernel(cols_ref, left_ref, m_ref, out_ref):
    shares = multiply(cols_ref, left_ref[...], m_ref)
    for y in range(Y):
        out_ref[y] = shares[y % 2]


def partial_kernel(cols_ref, own_ref, other_ref, m_ref, keep_ref, send_ref, list_ref):
    shares = multiply(cols_ref, picked(cols_ref, own_ref, other_ref, list_ref), m_ref)
    near = place()[3]
    keep_ref[...] = jnp.where(near == 0, *shares)
    send_ref[...] = jnp.where(near == 0, *shares[::-1])


def square_kernel(shares_ref, square_ref, half_ref):
    h = lax.rem(lax.axis_index("col") // (2 * C), 2)
    square_ref[...] = shares_ref[2 * h] + shares_ref[2 * h + 1]
    for pair in range(2):
        half_ref[pair] = (shares_ref[2 * pair] + shares_ref[2 * pair + 1]).astype(half_ref.dtype)


def final_kernel(cols_ref, keep_ref, both_ref, square_ref, out_ref):
    row, col, _, near = place()
    cube = keep_ref[...] + both_ref[1 - near]
    alive = cols_ref[row, col] >= 0
    out_ref[...] = jnp.where(alive, 3.0 * square_ref[...] - 2.0 * cube, 0.0).astype(out_ref.dtype)


def call(kernel, name, outs, arrays, scalars=(), grant=4, **options):
    vmem = pl.BlockSpec(memory_space=pltpu.VMEM)
    return pl.pallas_call(
        kernel,
        out_shape=[jax.ShapeDtypeStruct(shape, dtype) for shape, dtype in outs],
        in_specs=[pl.BlockSpec(memory_space=pltpu.SMEM)] * len(scalars) + [vmem] * len(arrays),
        out_specs=[vmem] * len(outs),
        compiler_params=pltpu.CompilerParams(vmem_limit_bytes=grant << 20),
        name=name,
        **options,
    )(*scalars, *arrays)


def gather(value, groups):
    return lax.all_gather(value, "col", axis=0, tiled=True, axis_index_groups=groups)


def exchange(value, axis, groups):
    return lax.all_to_all(value, axis, split_axis=0, concat_axis=0, tiled=True, axis_index_groups=groups)


def lines(line):
    own = gather(line, Z_LINES)
    return own, lax.ppermute(own, "col", SWAP)


def on_device(win_vals, couple_vals, win_cols):
    block, cols = (BS, BS), (win_cols,)
    lists = dict(scratch_shapes=[pltpu.SMEM((CLASS + 1,), jnp.int32)])
    flops = lambda count: pl.CostEstimate(flops=count * BS**3, bytes_accessed=4 << 20, transcendentals=0)
    shares = [(block, jnp.float32)] * 2

    packed = pack(win_cols, couple_vals[0, 0])
    (line,) = call(copies_kernel, "copies", [((Y,) + block, jnp.bfloat16)], (win_vals[0],))
    line = exchange(line, "col", Y_LINES)
    line, packed = lax.optimization_barrier((line, packed))
    held = exchange(packed.reshape((2 * BANDS, CLASS) + block), ("row", "col"), SPREAD)
    held = held.reshape(2, BANDS * CLASS * BS, BS)
    (line,) = call(choose_kernel, "choose", [((2,) + block, jnp.bfloat16)], (line,), cols)
    left = [((BS, BANDS * CLASS * BS), jnp.bfloat16)]
    (left,) = call(pick_kernel, "pick", left, lines(line), cols, 8, **lists)
    outs = [((Y,) + block, jnp.float32)]
    (sums,) = call(multiply_kernel, "multiply", outs, (left, held), cols, 16, cost_estimate=flops(128))

    outs = [(block, jnp.float32), ((2,) + block, jnp.bfloat16)]
    square, half = call(square_kernel, "square", outs, (exchange(sums, "col", Y_LINES),))

    line = lines(half)
    keep, send = call(partial_kernel, "partials", shares, (*line, held), cols, 16, cost_estimate=flops(128), **lists)
    outs = [(block, jnp.bfloat16)]
    (purified,) = call(final_kernel, "final", outs, (keep, gather(send[None], Y_NEAR), square), cols)
    return purified[None, None]


def solution(mesh):
    return jax.shard_map(
        on_device,
        mesh=mesh,
        in_specs=(P("row", "col", None, None), P("row", "col", None, None, None, None), P()),
        out_specs=P("row", "col", None, None),
        check_vma=False,
    )
```

```python
import jax
import jax.numpy as jnp
from jax import lax
from jax.experimental import pallas as pl
from jax.experimental.pallas import tpu as pltpu
from jax.sharding import PartitionSpec as P

BS = 128
BANDS = 8
GROUP = 12
LIVE = 8
Z, Y, C = 12, 4, 2
N_COL = Z * Y * C
QUADS = 2 * Z

CLASS = LIVE // 2
STEP = 4


def col_of(z, y, c):
    return (z * Y + y) * C + c


Y_LINES = [[col_of(z, y, c) for y in range(Y)] for z in range(Z) for c in range(C)]
Y_NEAR = [[col_of(z, 2 * h + p, c) for p in range(2)] for z in range(Z) for h in range(2) for c in range(C)]
Z_LINES = [[col_of(z, y, (z + c) % C) for z in range(Z)] for y in range(Y) for c in range(C)]
SWAP = [(s, s ^ 1) for s in range(N_COL)]
Y_OTHERS = [[(s, s ^ step * C) for s in range(N_COL)] for step in (1, 2, 3)]
SPREAD = [[row * N_COL + col for col in pair for row in range(BANDS)] for pair in Y_NEAR]


def place():
    col = lax.axis_index("col")
    return lax.axis_index("row"), col, lax.rem(col, C), lax.rem(col // C, 2)


def pair_alive(cols_ref, window, first):
    return [cols_ref[window, first + p * C] >= 0 for p in range(2)]


def member_of(alive, k):
    return jnp.where(alive[0] & alive[1], k, jnp.where(alive[0], 0, 1))


def list_live(cols_ref, list_ref, window, band, k, value):
    count, singles = jnp.int32(0), jnp.int32(0)
    for n in range(GROUP // 2):
        quad, core = divmod(n, C)
        alive = pair_alive(cols_ref, window, band * GROUP + quad * 4 + core)
        single = alive[0] != alive[1]
        taken = (alive[0] & alive[1]) | (single & (lax.rem(singles, 2) == k))
        list_ref[jnp.minimum(count, CLASS)] = value(quad, core, member_of(alive, k))
        count = count + taken.astype(jnp.int32)
        singles = singles + single.astype(jnp.int32)
    return count


def pack_kernel(cols_ref, couple_ref, out_ref, lists):
    band = lax.axis_index("row")
    for i in range(STEP):
        for k in range(2):
            slots = lists.at[i * 2 + k]
            count = list_live(
                cols_ref, slots, pl.program_id(0) * STEP + i, band, k, lambda quad, core, p: quad * 4 + p * C + core
            )
            for j in range(CLASS):
                out_ref[k, i, j] = couple_ref[i, jnp.where(j < count, slots[j], 0)]


def pack(win_cols, couple):
    return pl.pallas_call(
        pack_kernel,
        out_shape=jax.ShapeDtypeStruct((2, BANDS, CLASS, BS, BS), couple.dtype),
        grid=(BANDS // STEP,),
        in_specs=[
            pl.BlockSpec(memory_space=pltpu.SMEM),
            pl.BlockSpec((STEP, GROUP, BS, BS), lambda i: (i, 0, 0, 0)),
        ],
        out_specs=pl.BlockSpec((2, STEP, CLASS, BS, BS), lambda i: (0, i, 0, 0, 0)),
        scratch_shapes=[pltpu.SMEM((2 * STEP, CLASS + 1), jnp.int32)],
        cost_estimate=pl.CostEstimate(flops=0, bytes_accessed=5 << 20, transcendentals=0),
        compiler_params=pltpu.CompilerParams(vmem_limit_bytes=56 << 20),
        name="pack",
    )(win_cols, couple)


def choose_kernel(cols_ref, mine_ref, theirs_ref, far_mine_ref, far_theirs_ref, out_ref):
    row, col, core, near = place()
    here = col - near * C
    pairs = ((here, mine_ref, theirs_ref), (here ^ 2 * C, far_mine_ref, far_theirs_ref))
    for n, (first, same_ref, other_ref) in enumerate(pairs):
        alive = pair_alive(cols_ref, row, first)
        out_ref[n] = jnp.where(member_of(alive, near) == near, same_ref[...], other_ref[...])


def picked(cols_ref, own_ref, other_ref, list_ref):
    row, col, core, near = place()
    line, half = lax.rem(col // (Y * C) + core, 2), lax.rem(col // (2 * C), 2)
    picks = []
    for band in range(BANDS):
        def where(quad, c, _, band=band):
            z, h = divmod(band * 3 + quad, 2)
            return z * 2 + lax.rem(half + h, 2) + QUADS * lax.rem(line + c + z, 2)

        count = list_live(cols_ref, list_ref, row, band, near, where)
        for j in range(CLASS):
            at = jnp.where(j < count, list_ref[j], 0)
            inside = lax.rem(at, QUADS)
            block = jnp.where(at < QUADS, own_ref[inside], other_ref[inside])
            picks.append(jnp.where(j < count, block, jnp.zeros_like(block)))
    return jnp.concatenate(picks, axis=1)


def multiply(cols_ref, left, m_ref):
    row, col, _, near = place()
    alive = pair_alive(cols_ref, row, col - near * C)
    chosen = [m_ref[member_of(alive, k)] for k in range(2)]
    product = jnp.dot(left, jnp.concatenate(chosen, axis=1), preferred_element_type=jnp.float32)
    return product[:, :BS], product[:, BS:]


def pick_kernel(cols_ref, own_ref, other_ref, left_ref, list_ref):
    left_ref[...] = picked(cols_ref, own_ref, other_ref, list_ref)


def multiply_kernel(cols_ref, left_ref, m_ref, out_ref):
    shares = multiply(cols_ref, left_ref[...], m_ref)
    for y in range(Y):
        out_ref[y] = shares[y % 2]


def partial_kernel(cols_ref, own_ref, other_ref, m_ref, keep_ref, send_ref, list_ref):
    shares = multiply(cols_ref, picked(cols_ref, own_ref, other_ref, list_ref), m_ref)
    near = place()[3]
    keep_ref[...] = jnp.where(near == 0, *shares)
    send_ref[...] = jnp.where(near == 0, *shares[::-1])


def square_kernel(shares_ref, square_ref, half_ref):
    h = lax.rem(lax.axis_index("col") // (2 * C), 2)
    totals = [shares_ref[2 * pair] + shares_ref[2 * pair + 1] for pair in (h, 1 - h)]
    square_ref[...] = totals[0]
    for pair in range(2):
        half_ref[pair] = totals[pair].astype(half_ref.dtype)


def final_kernel(cols_ref, keep_ref, both_ref, square_ref, out_ref):
    row, col, _, near = place()
    cube = keep_ref[...] + both_ref[1 - near]
    alive = cols_ref[row, col] >= 0
    out_ref[...] = jnp.where(alive, 3.0 * square_ref[...] - 2.0 * cube, 0.0).astype(out_ref.dtype)


def call(kernel, name, outs, arrays, scalars=(), grant=4, **options):
    vmem = pl.BlockSpec(memory_space=pltpu.VMEM)
    return pl.pallas_call(
        kernel,
        out_shape=[jax.ShapeDtypeStruct(shape, dtype) for shape, dtype in outs],
        in_specs=[pl.BlockSpec(memory_space=pltpu.SMEM)] * len(scalars) + [vmem] * len(arrays),
        out_specs=[vmem] * len(outs),
        compiler_params=pltpu.CompilerParams(vmem_limit_bytes=grant << 20),
        name=name,
        **options,
    )(*scalars, *arrays)


def gather(value, groups):
    return lax.all_gather(value, "col", axis=0, tiled=True, axis_index_groups=groups)


def exchange(value, axis, groups):
    return lax.all_to_all(value, axis, split_axis=0, concat_axis=0, tiled=True, axis_index_groups=groups)


def lines(line):
    own = gather(line, Z_LINES)
    return own, lax.ppermute(own, "col", SWAP)


def on_device(win_vals, couple_vals, win_cols):
    block, cols = (BS, BS), (win_cols,)
    lists = dict(scratch_shapes=[pltpu.SMEM((CLASS + 1,), jnp.int32)])
    flops = lambda count: pl.CostEstimate(flops=count * BS**3, bytes_accessed=4 << 20, transcendentals=0)
    shares = [(block, jnp.float32)] * 2

    x = win_vals[0, 0]
    others = [lax.ppermute(x, "col", route) for route in Y_OTHERS]
    packed = pack(win_cols, couple_vals[0, 0])
    *others, packed = lax.optimization_barrier((*others, packed))
    held = exchange(packed.reshape((2 * BANDS, CLASS) + block), ("row", "col"), SPREAD)
    held = held.reshape(2, BANDS * CLASS * BS, BS)
    (line,) = call(choose_kernel, "choose", [((2,) + block, jnp.bfloat16)], (x, *others), cols)
    left = [((BS, BANDS * CLASS * BS), jnp.bfloat16)]
    (left,) = call(pick_kernel, "pick", left, lines(line), cols, 8, **lists)
    outs = [((Y,) + block, jnp.float32)]
    (sums,) = call(multiply_kernel, "multiply", outs, (left, held), cols, 16, cost_estimate=flops(128))

    outs = [(block, jnp.float32), ((2,) + block, jnp.bfloat16)]
    square, half = call(square_kernel, "square", outs, (exchange(sums, "col", Y_LINES),))

    line = lines(half)
    keep, send = call(partial_kernel, "partials", shares, (*line, held), cols, 16, cost_estimate=flops(128), **lists)
    outs = [(block, jnp.bfloat16)]
    (purified,) = call(final_kernel, "final", outs, (keep, gather(send[None], Y_NEAR), square), cols)
    return purified[None, None]


def solution(mesh):
    return jax.shard_map(
        on_device,
        mesh=mesh,
        in_specs=(P("row", "col", None, None), P("row", "col", None, None, None, None), P()),
        out_specs=P("row", "col", None, None),
        check_vma=False,
    )
```

```python
import jax
import jax.numpy as jnp
from jax import lax
from jax.experimental import pallas as pl
from jax.experimental.pallas import tpu as pltpu
from jax.sharding import PartitionSpec as P

BS = 128
BANDS = 8
GROUP = 12
LIVE = 8
Z, Y, C = 12, 4, 2
N_COL = Z * Y * C
QUADS = 2 * Z

CLASS = LIVE // 2
STEP = 4


def col_of(z, y, c):
    return (z * Y + y) * C + c


Y_LINES = [[col_of(z, y, c) for y in range(Y)] for z in range(Z) for c in range(C)]
Y_FAR = [[col_of(z, 2 * h + p, c) for h in range(2)] for z in range(Z) for p in range(2) for c in range(C)]
Y_NEAR = [[col_of(z, 2 * h + p, c) for p in range(2)] for z in range(Z) for h in range(2) for c in range(C)]
Z_LINES = [[col_of(z, y, (z + c) % C) for z in range(Z)] for y in range(Y) for c in range(C)]
SWAP = [(s, s ^ 1) for s in range(N_COL)]
SPREAD = [[row * N_COL + col for col in pair for row in range(BANDS)] for pair in Y_NEAR]


def place():
    col = lax.axis_index("col")
    return lax.axis_index("row"), col, lax.rem(col, C), lax.rem(col // C, 2)


def pair_alive(cols_ref, window, first):
    return [cols_ref[window, first + p * C] >= 0 for p in range(2)]


def member_of(alive, k):
    return jnp.where(alive[0] & alive[1], k, jnp.where(alive[0], 0, 1))


def list_live(cols_ref, list_ref, window, band, k, value):
    count, singles = jnp.int32(0), jnp.int32(0)
    for n in range(GROUP // 2):
        quad, core = divmod(n, C)
        alive = pair_alive(cols_ref, window, band * GROUP + quad * 4 + core)
        single = alive[0] != alive[1]
        taken = (alive[0] & alive[1]) | (single & (lax.rem(singles, 2) == k))
        list_ref[jnp.minimum(count, CLASS)] = value(quad, core, member_of(alive, k))
        count = count + taken.astype(jnp.int32)
        singles = singles + single.astype(jnp.int32)
    return count


def pack_kernel(cols_ref, couple_ref, out_ref, lists):
    band = lax.axis_index("row")
    for i in range(STEP):
        for k in range(2):
            slots = lists.at[i * 2 + k]
            count = list_live(
                cols_ref, slots, pl.program_id(0) * STEP + i, band, k, lambda quad, core, p: quad * 4 + p * C + core
            )
            for j in range(CLASS):
                out_ref[k, i, j] = couple_ref[i, jnp.where(j < count, slots[j], 0)]


def pack(win_cols, couple):
    return pl.pallas_call(
        pack_kernel,
        out_shape=jax.ShapeDtypeStruct((2, BANDS, CLASS, BS, BS), couple.dtype),
        grid=(BANDS // STEP,),
        in_specs=[
            pl.BlockSpec(memory_space=pltpu.SMEM),
            pl.BlockSpec((STEP, GROUP, BS, BS), lambda i: (i, 0, 0, 0)),
        ],
        out_specs=pl.BlockSpec((2, STEP, CLASS, BS, BS), lambda i: (0, i, 0, 0, 0)),
        scratch_shapes=[pltpu.SMEM((2 * STEP, CLASS + 1), jnp.int32)],
        cost_estimate=pl.CostEstimate(flops=0, bytes_accessed=5 << 20, transcendentals=0),
        compiler_params=pltpu.CompilerParams(vmem_limit_bytes=56 << 20),
        name="pack",
    )(win_cols, couple)


def copies_kernel(x_ref, out_ref):
    for y in range(Y):
        out_ref[y] = x_ref[0]


def choose_kernel(cols_ref, line_ref, out_ref):
    row, col, core, near = place()
    first = col // (Y * C) * (Y * C) + core
    for h in range(2):
        alive = pair_alive(cols_ref, row, first + 2 * h * C)
        out_ref[h] = line_ref[2 * h + member_of(alive, near)]


def list_picks(cols_ref, list_ref, picks_ref):
    row, col, core, near = place()
    line = lax.rem(col // (Y * C) + core, 2)
    for band in range(BANDS):
        where = lambda quad, c, _, band=band: (
            band * 3 + quad + QUADS * lax.rem(line + c + (band * 3 + quad) // 2, 2)
        )
        count = list_live(cols_ref, list_ref, row, band, near, where)
        for j in range(CLASS):
            picks_ref[band * CLASS + j] = jnp.where(j < count, list_ref[j], -1)


def picked(picks_ref, own_ref, other_ref):
    blocks = []
    for n in range(BANDS * CLASS):
        pick = picks_ref[n]
        inside = lax.rem(jnp.maximum(pick, 0), QUADS)
        block = jnp.where(pick < QUADS, own_ref[inside], other_ref[inside])
        blocks.append(jnp.where(pick >= 0, block, jnp.zeros_like(block)))
    return jnp.concatenate(blocks, axis=1)


def multiply(cols_ref, left, m_ref):
    row, col, _, near = place()
    alive = pair_alive(cols_ref, row, col - near * C)
    chosen = [m_ref[member_of(alive, k)] for k in range(2)]
    product = jnp.dot(left, jnp.concatenate(chosen, axis=1), preferred_element_type=jnp.float32)
    return product[:, :BS], product[:, BS:]


def pick_kernel(cols_ref, own_ref, other_ref, left_ref, picks_ref, list_ref):
    list_picks(cols_ref, list_ref, picks_ref)
    left_ref[...] = picked(picks_ref, own_ref, other_ref)


def share(keep_ref, send_ref, shares):
    near = place()[3]
    keep_ref[...] = jnp.where(near == 0, *shares)
    send_ref[0] = jnp.where(near == 0, *shares[::-1])


def multiply_kernel(cols_ref, left_ref, m_ref, keep_ref, send_ref):
    share(keep_ref, send_ref, multiply(cols_ref, left_ref[...], m_ref))


def partial_kernel(cols_ref, picks_ref, own_ref, other_ref, m_ref, keep_ref, send_ref):
    share(keep_ref, send_ref, multiply(cols_ref, picked(picks_ref, own_ref, other_ref), m_ref))


def square_kernel(keep_ref, both_ref, square_ref, half_ref):
    total = keep_ref[...] + both_ref[1 - place()[3]]
    square_ref[...] = total
    half_ref[0] = total.astype(half_ref.dtype)


def final_kernel(cols_ref, keep_ref, both_ref, square_ref, out_ref):
    row, col, _, near = place()
    cube = keep_ref[...] + both_ref[1 - near]
    alive = cols_ref[row, col] >= 0
    out_ref[...] = jnp.where(alive, 3.0 * square_ref[...] - 2.0 * cube, 0.0).astype(out_ref.dtype)


def call(kernel, name, outs, arrays, scalars=(), grant=4, **options):
    smem, vmem = (pl.BlockSpec(memory_space=space) for space in (pltpu.SMEM, pltpu.VMEM))
    return pl.pallas_call(
        kernel,
        out_shape=[jax.ShapeDtypeStruct(shape, dtype) for shape, dtype in outs],
        in_specs=[smem] * len(scalars) + [vmem] * len(arrays),
        out_specs=[smem if dtype == jnp.int32 else vmem for _, dtype in outs],
        compiler_params=pltpu.CompilerParams(vmem_limit_bytes=grant << 20),
        name=name,
        **options,
    )(*scalars, *arrays)


def gather(value, groups):
    return lax.all_gather(value, "col", axis=0, tiled=True, axis_index_groups=groups)


def exchange(value, axis, groups):
    return lax.all_to_all(value, axis, split_axis=0, concat_axis=0, tiled=True, axis_index_groups=groups)


def lines(line):
    own = gather(line, Z_LINES)
    return own, lax.ppermute(own, "col", SWAP)


def on_device(win_vals, couple_vals, win_cols):
    block, cols = (BS, BS), (win_cols,)
    lists = dict(scratch_shapes=[pltpu.SMEM((CLASS + 1,), jnp.int32)])
    flops = lambda count: pl.CostEstimate(flops=count * BS**3, bytes_accessed=4 << 20, transcendentals=0)
    shares = [(block, jnp.float32), ((1,) + block, jnp.float32)]

    packed = pack(win_cols, couple_vals[0, 0])
    (line,) = call(copies_kernel, "copies", [((Y,) + block, jnp.bfloat16)], (win_vals[0],))
    line = exchange(line, "col", Y_LINES)
    line, packed = lax.optimization_barrier((line, packed))
    held = exchange(packed.reshape((2 * BANDS, CLASS) + block), ("row", "col"), SPREAD)
    held = held.reshape(2, BANDS * CLASS * BS, BS)
    (line,) = call(choose_kernel, "choose", [((2,) + block, jnp.bfloat16)], (line,), cols)
    outs = [((BS, BANDS * CLASS * BS), jnp.bfloat16), ((BANDS * CLASS,), jnp.int32)]
    left, picks = call(pick_kernel, "pick", outs, lines(line), cols, 8, **lists)
    keep, send = call(multiply_kernel, "multiply", shares, (left, held), cols, 16, cost_estimate=flops(128))

    outs = [(block, jnp.float32), ((1,) + block, jnp.bfloat16)]
    square, half = call(square_kernel, "square", outs, (keep, gather(send, Y_NEAR)))

    line = lines(gather(half, Y_FAR))
    scalars = (win_cols, picks)
    keep, send = call(partial_kernel, "partials", shares, (*line, held), scalars, 16, cost_estimate=flops(128))
    outs = [(block, jnp.bfloat16)]
    (purified,) = call(final_kernel, "final", outs, (keep, gather(send, Y_NEAR), square), cols)
    return purified[None, None]


def solution(mesh):
    return jax.shard_map(
        on_device,
        mesh=mesh,
        in_specs=(P("row", "col", None, None), P("row", "col", None, None, None, None), P()),
        out_specs=P("row", "col", None, None),
        check_vma=False,
    )
```

```python
import jax
import jax.numpy as jnp
from jax import lax
from jax.experimental import pallas as pl
from jax.experimental.pallas import tpu as pltpu
from jax.sharding import PartitionSpec as P

BS = 128
BANDS = 8
GROUP = 12
LIVE = 8
Z, Y, C = 12, 4, 2
N_COL = Z * Y * C
QUADS = 2 * Z

CLASS = LIVE // 2
STEP = 4


def col_of(z, y, c):
    return (z * Y + y) * C + c


Y_LINES = [[col_of(z, y, c) for y in range(Y)] for z in range(Z) for c in range(C)]
Y_NEAR = [[col_of(z, 2 * h + p, c) for p in range(2)] for z in range(Z) for h in range(2) for c in range(C)]
Z_LINES = [[col_of(z, y, (z + c) % C) for z in range(Z)] for y in range(Y) for c in range(C)]
SWAP = [(s, s ^ 1) for s in range(N_COL)]
SPREAD = [[row * N_COL + col for col in pair for row in range(BANDS)] for pair in Y_NEAR]


def place():
    col = lax.axis_index("col")
    return lax.axis_index("row"), col, lax.rem(col, C), lax.rem(col // C, 2)


def pair_alive(cols_ref, window, first):
    return [cols_ref[window, first + p * C] >= 0 for p in range(2)]


def member_of(alive, k):
    return jnp.where(alive[0] & alive[1], k, jnp.where(alive[0], 0, 1))


def list_live(cols_ref, list_ref, window, band, k, value):
    count, singles = jnp.int32(0), jnp.int32(0)
    for n in range(GROUP // 2):
        quad, core = divmod(n, C)
        alive = pair_alive(cols_ref, window, band * GROUP + quad * 4 + core)
        single = alive[0] != alive[1]
        taken = (alive[0] & alive[1]) | (single & (lax.rem(singles, 2) == k))
        list_ref[jnp.minimum(count, CLASS)] = value(quad, core, member_of(alive, k))
        count = count + taken.astype(jnp.int32)
        singles = singles + single.astype(jnp.int32)
    return count


def pack_kernel(cols_ref, couple_ref, out_ref, lists):
    band = lax.axis_index("row")
    for i in range(STEP):
        for k in range(2):
            slots = lists.at[i * 2 + k]
            count = list_live(
                cols_ref, slots, pl.program_id(0) * STEP + i, band, k, lambda quad, core, p: quad * 4 + p * C + core
            )
            for j in range(CLASS):
                out_ref[k, i, j] = couple_ref[i, jnp.where(j < count, slots[j], 0)]


def pack(win_cols, couple):
    return pl.pallas_call(
        pack_kernel,
        out_shape=jax.ShapeDtypeStruct((2, BANDS, CLASS, BS, BS), couple.dtype),
        grid=(BANDS // STEP,),
        in_specs=[
            pl.BlockSpec(memory_space=pltpu.SMEM),
            pl.BlockSpec((STEP, GROUP, BS, BS), lambda i: (i, 0, 0, 0)),
        ],
        out_specs=pl.BlockSpec((2, STEP, CLASS, BS, BS), lambda i: (0, i, 0, 0, 0)),
        scratch_shapes=[pltpu.SMEM((2 * STEP, CLASS + 1), jnp.int32)],
        cost_estimate=pl.CostEstimate(flops=0, bytes_accessed=5 << 20, transcendentals=0),
        compiler_params=pltpu.CompilerParams(vmem_limit_bytes=56 << 20),
        name="pack",
    )(win_cols, couple)


def copies_kernel(x_ref, out_ref):
    for y in range(Y):
        out_ref[y] = x_ref[0]


def choose_kernel(cols_ref, line_ref, out_ref):
    row, col, core, near = place()
    first = col // (Y * C) * (Y * C) + core
    for h in range(2):
        alive = pair_alive(cols_ref, row, first + 2 * h * C)
        out_ref[h] = line_ref[2 * h + member_of(alive, near)]


def list_picks(cols_ref, list_ref, picks_ref):
    row, col, core, near = place()
    line = lax.rem(col // (Y * C) + core, 2)
    for band in range(BANDS):
        where = lambda quad, c, _, band=band: (
            band * 3 + quad + QUADS * lax.rem(line + c + (band * 3 + quad) // 2, 2)
        )
        count = list_live(cols_ref, list_ref, row, band, near, where)
        for j in range(CLASS):
            picks_ref[band * CLASS + j] = jnp.where(j < count, list_ref[j], -1)


def picked(picks_ref, own_ref, other_ref):
    blocks = []
    for n in range(BANDS * CLASS):
        pick = picks_ref[n]
        inside = lax.rem(jnp.maximum(pick, 0), QUADS)
        block = jnp.where(pick < QUADS, own_ref[inside], other_ref[inside])
        blocks.append(jnp.where(pick >= 0, block, jnp.zeros_like(block)))
    return jnp.concatenate(blocks, axis=1)


def multiply(cols_ref, left, m_ref):
    row, col, _, near = place()
    alive = pair_alive(cols_ref, row, col - near * C)
    chosen = [m_ref[member_of(alive, k)] for k in range(2)]
    product = jnp.dot(left, jnp.concatenate(chosen, axis=1), preferred_element_type=jnp.float32)
    return product[:, :BS], product[:, BS:]


def pick_kernel(cols_ref, own_ref, other_ref, left_ref, picks_ref, list_ref):
    list_picks(cols_ref, list_ref, picks_ref)
    left_ref[...] = picked(picks_ref, own_ref, other_ref)


def multiply_kernel(cols_ref, left_ref, m_ref, out_ref):
    shares = multiply(cols_ref, left_ref[...], m_ref)
    for y in range(Y):
        out_ref[y] = shares[y % 2]


def partial_kernel(cols_ref, picks_ref, own_ref, other_ref, m_ref, keep_ref, send_ref):
    shares = multiply(cols_ref, picked(picks_ref, own_ref, other_ref), m_ref)
    near = place()[3]
    keep_ref[...] = jnp.where(near == 0, *shares)
    send_ref[...] = jnp.where(near == 0, *shares[::-1])


def square_kernel(shares_ref, square_ref, half_ref):
    h = lax.rem(lax.axis_index("col") // (2 * C), 2)
    square_ref[...] = shares_ref[2 * h] + shares_ref[2 * h + 1]
    for pair in range(2):
        half_ref[pair] = (shares_ref[2 * pair] + shares_ref[2 * pair + 1]).astype(half_ref.dtype)


def final_kernel(cols_ref, keep_ref, both_ref, square_ref, out_ref):
    row, col, _, near = place()
    cube = keep_ref[...] + both_ref[1 - near]
    alive = cols_ref[row, col] >= 0
    out_ref[...] = jnp.where(alive, 3.0 * square_ref[...] - 2.0 * cube, 0.0).astype(out_ref.dtype)


def call(kernel, name, outs, arrays, scalars=(), grant=4, **options):
    smem, vmem = (pl.BlockSpec(memory_space=space) for space in (pltpu.SMEM, pltpu.VMEM))
    return pl.pallas_call(
        kernel,
        out_shape=[jax.ShapeDtypeStruct(shape, dtype) for shape, dtype in outs],
        in_specs=[smem] * len(scalars) + [vmem] * len(arrays),
        out_specs=[smem if dtype == jnp.int32 else vmem for _, dtype in outs],
        compiler_params=pltpu.CompilerParams(vmem_limit_bytes=grant << 20),
        name=name,
        **options,
    )(*scalars, *arrays)


def gather(value, groups):
    return lax.all_gather(value, "col", axis=0, tiled=True, axis_index_groups=groups)


def exchange(value, axis, groups):
    return lax.all_to_all(value, axis, split_axis=0, concat_axis=0, tiled=True, axis_index_groups=groups)


def lines(line):
    own = gather(line, Z_LINES)
    return own, lax.ppermute(own, "col", SWAP)


def on_device(win_vals, couple_vals, win_cols):
    block, cols = (BS, BS), (win_cols,)
    lists = dict(scratch_shapes=[pltpu.SMEM((CLASS + 1,), jnp.int32)])
    flops = lambda count: pl.CostEstimate(flops=count * BS**3, bytes_accessed=4 << 20, transcendentals=0)
    shares = [(block, jnp.float32)] * 2

    packed = pack(win_cols, couple_vals[0, 0])
    (line,) = call(copies_kernel, "copies", [((Y,) + block, jnp.bfloat16)], (win_vals[0],))
    line = exchange(line, "col", Y_LINES)
    line, packed = lax.optimization_barrier((line, packed))
    held = exchange(packed.reshape((2 * BANDS, CLASS) + block), ("row", "col"), SPREAD)
    held = held.reshape(2, BANDS * CLASS * BS, BS)
    (line,) = call(choose_kernel, "choose", [((2,) + block, jnp.bfloat16)], (line,), cols)
    outs = [((BS, BANDS * CLASS * BS), jnp.bfloat16), ((BANDS * CLASS,), jnp.int32)]
    left, picks = call(pick_kernel, "pick", outs, lines(line), cols, 8, **lists)
    outs = [((Y,) + block, jnp.float32)]
    (sums,) = call(multiply_kernel, "multiply", outs, (left, held), cols, 16, cost_estimate=flops(128))

    outs = [(block, jnp.float32), ((2,) + block, jnp.bfloat16)]
    square, half = call(square_kernel, "square", outs, (exchange(sums, "col", Y_LINES),))

    line = lines(half)
    scalars = (win_cols, picks)
    keep, send = call(partial_kernel, "partials", shares, (*line, held), scalars, 16, cost_estimate=flops(128))
    outs = [(block, jnp.bfloat16)]
    (purified,) = call(final_kernel, "final", outs, (keep, gather(send[None], Y_NEAR), square), cols)
    return purified[None, None]


def solution(mesh):
    return jax.shard_map(
        on_device,
        mesh=mesh,
        in_specs=(P("row", "col", None, None), P("row", "col", None, None, None, None), P()),
        out_specs=P("row", "col", None, None),
        check_vma=False,
    )
```

```python
import jax
import jax.numpy as jnp
from jax import lax
from jax.experimental import pallas as pl
from jax.experimental.pallas import tpu as pltpu
from jax.sharding import PartitionSpec as P

BS = 128
BANDS = 8
GROUP = 12
LIVE = 8
Z, Y, C = 12, 4, 2
N_COL = Z * Y * C
QUADS = 2 * Z

CLASS = LIVE // 2
STEP = 4


def col_of(z, y, c):
    return (z * Y + y) * C + c


Y_LINES = [[col_of(z, y, c) for y in range(Y)] for z in range(Z) for c in range(C)]
Y_NEAR = [[col_of(z, 2 * h + p, c) for p in range(2)] for z in range(Z) for h in range(2) for c in range(C)]
Z_LINES = [[col_of(z, y, (z + c) % C) for z in range(Z)] for y in range(Y) for c in range(C)]
SWAP = [(s, s ^ 1) for s in range(N_COL)]
SPREAD = [[row * N_COL + col for col in pair for row in range(BANDS)] for pair in Y_NEAR]


def place():
    col = lax.axis_index("col")
    return lax.axis_index("row"), col, lax.rem(col, C), lax.rem(col // C, 2)


def pair_alive(cols_ref, window, first):
    return [cols_ref[window, first + p * C] >= 0 for p in range(2)]


def member_of(alive, k):
    return jnp.where(alive[0] & alive[1], k, jnp.where(alive[0], 0, 1))


def list_live(cols_ref, list_ref, window, band, k, value):
    count, singles = jnp.int32(0), jnp.int32(0)
    for n in range(GROUP // 2):
        quad, core = divmod(n, C)
        alive = pair_alive(cols_ref, window, band * GROUP + quad * 4 + core)
        single = alive[0] != alive[1]
        taken = (alive[0] & alive[1]) | (single & (lax.rem(singles, 2) == k))
        list_ref[jnp.minimum(count, CLASS)] = value(quad, core, member_of(alive, k))
        count = count + taken.astype(jnp.int32)
        singles = singles + single.astype(jnp.int32)
    return count


def list_both(cols_ref, lists, window, band):
    counts, singles = [jnp.int32(0)] * 2, jnp.int32(0)
    for n in range(GROUP // 2):
        quad, core = divmod(n, C)
        slot = quad * 4 + core
        alive = [a.astype(jnp.int32) for a in pair_alive(cols_ref, window, band * GROUP + slot)]
        both, single = alive[0] & alive[1], alive[0] ^ alive[1]
        lists[0, jnp.minimum(counts[0], CLASS)] = slot + C * (1 - alive[0])
        lists[1, jnp.minimum(counts[1], CLASS)] = slot + C * alive[1]
        odd = singles & 1
        counts[0] = counts[0] + (both | (single & (1 - odd)))
        counts[1] = counts[1] + (both | (single & odd))
        singles = singles + single
    return counts


def pack_kernel(cols_ref, couple_ref, out_ref, lists):
    band = lax.axis_index("row")
    for i in range(STEP):
        slots = lists.at[i]
        counts = list_both(cols_ref, slots, pl.program_id(0) * STEP + i, band)
        for k in range(2):
            for j in range(CLASS):
                out_ref[k, i, j] = couple_ref[i, jnp.where(j < counts[k], slots[k, j], 0)]


def pack(win_cols, couple):
    return pl.pallas_call(
        pack_kernel,
        out_shape=jax.ShapeDtypeStruct((2, BANDS, CLASS, BS, BS), couple.dtype),
        grid=(BANDS // STEP,),
        in_specs=[
            pl.BlockSpec(memory_space=pltpu.SMEM),
            pl.BlockSpec((STEP, GROUP, BS, BS), lambda i: (i, 0, 0, 0)),
        ],
        out_specs=pl.BlockSpec((2, STEP, CLASS, BS, BS), lambda i: (0, i, 0, 0, 0)),
        scratch_shapes=[pltpu.SMEM((STEP, 2, CLASS + 1), jnp.int32)],
        cost_estimate=pl.CostEstimate(flops=0, bytes_accessed=5 << 20, transcendentals=0),
        compiler_params=pltpu.CompilerParams(vmem_limit_bytes=56 << 20),
        name="pack",
    )(win_cols, couple)


def copies_kernel(x_ref, out_ref):
    for y in range(Y):
        out_ref[y] = x_ref[0]


def choose_kernel(cols_ref, line_ref, out_ref):
    row, col, core, near = place()
    first = col // (Y * C) * (Y * C) + core
    for h in range(2):
        alive = pair_alive(cols_ref, row, first + 2 * h * C)
        out_ref[h] = line_ref[2 * h + member_of(alive, near)]


def list_picks(cols_ref, list_ref, picks_ref):
    row, col, core, near = place()
    line = lax.rem(col // (Y * C) + core, 2)
    for band in range(BANDS):
        where = lambda quad, c, _, band=band: (
            band * 3 + quad + QUADS * lax.rem(line + c + (band * 3 + quad) // 2, 2)
        )
        count = list_live(cols_ref, list_ref, row, band, near, where)
        for j in range(CLASS):
            picks_ref[band * CLASS + j] = jnp.where(j < count, list_ref[j], -1)


def picked(picks_ref, own_ref, other_ref):
    blocks = []
    for n in range(BANDS * CLASS):
        pick = picks_ref[n]
        inside = lax.rem(jnp.maximum(pick, 0), QUADS)
        block = jnp.where(pick < QUADS, own_ref[inside], other_ref[inside])
        blocks.append(jnp.where(pick >= 0, block, jnp.zeros_like(block)))
    return jnp.concatenate(blocks, axis=1)


def multiply(cols_ref, left, m_ref):
    row, col, _, near = place()
    alive = pair_alive(cols_ref, row, col - near * C)
    chosen = [m_ref[member_of(alive, k)] for k in range(2)]
    product = jnp.dot(left, jnp.concatenate(chosen, axis=1), preferred_element_type=jnp.float32)
    return product[:, :BS], product[:, BS:]


def pick_kernel(cols_ref, own_ref, other_ref, left_ref, weights_ref, picks_ref, list_ref):
    near = place()[3]
    for p in range(2):
        weights_ref[p] = jnp.full((1, BS), (near != p).astype(jnp.float32))
    list_picks(cols_ref, list_ref, picks_ref)
    left_ref[...] = picked(picks_ref, own_ref, other_ref)


def multiply_kernel(cols_ref, left_ref, m_ref, out_ref):
    shares = multiply(cols_ref, left_ref[...], m_ref)
    for y in range(Y):
        out_ref[y] = shares[y % 2]


def partial_kernel(cols_ref, picks_ref, own_ref, other_ref, m_ref, keep_ref, send_ref):
    shares = multiply(cols_ref, picked(picks_ref, own_ref, other_ref), m_ref)
    row, col, _, near = place()
    keep = jnp.where(near == 0, *shares)
    send = jnp.where(near == 0, *shares[::-1])
    keep_ref[...] = jnp.where(cols_ref[row, col] >= 0, keep, 0.0)
    send_ref[0] = jnp.where(cols_ref[row, col ^ C] >= 0, send, 0.0)


def square_kernel(cols_ref, shares_ref, square_ref, half_ref):
    row, col, _, _ = place()
    h = lax.rem(col // (2 * C), 2)
    total = shares_ref[2 * h] + shares_ref[2 * h + 1]
    square_ref[...] = jnp.where(cols_ref[row, col] >= 0, total, 0.0)
    for pair in range(2):
        half_ref[pair] = (shares_ref[2 * pair] + shares_ref[2 * pair + 1]).astype(half_ref.dtype)


def call(kernel, name, outs, arrays, scalars=(), grant=4, **options):
    smem, vmem = (pl.BlockSpec(memory_space=space) for space in (pltpu.SMEM, pltpu.VMEM))
    return pl.pallas_call(
        kernel,
        out_shape=[jax.ShapeDtypeStruct(shape, dtype) for shape, dtype in outs],
        in_specs=[smem] * len(scalars) + [vmem] * len(arrays),
        out_specs=[smem if dtype == jnp.int32 else vmem for _, dtype in outs],
        compiler_params=pltpu.CompilerParams(vmem_limit_bytes=grant << 20),
        name=name,
        **options,
    )(*scalars, *arrays)


def gather(value, groups):
    return lax.all_gather(value, "col", axis=0, tiled=True, axis_index_groups=groups)


def exchange(value, axis, groups):
    return lax.all_to_all(value, axis, split_axis=0, concat_axis=0, tiled=True, axis_index_groups=groups)


def lines(line):
    own = gather(line, Z_LINES)
    return own, lax.ppermute(own, "col", SWAP)


def on_device(win_vals, couple_vals, win_cols):
    block, cols = (BS, BS), (win_cols,)
    lists = dict(scratch_shapes=[pltpu.SMEM((CLASS + 1,), jnp.int32)])
    flops = lambda count: pl.CostEstimate(flops=count * BS**3, bytes_accessed=4 << 20, transcendentals=0)
    shares = [(block, jnp.float32), ((1,) + block, jnp.float32)]

    packed = pack(win_cols, couple_vals[0, 0])
    (line,) = call(copies_kernel, "copies", [((Y,) + block, jnp.bfloat16)], (win_vals[0],))
    line = exchange(line, "col", Y_LINES)
    line, packed = lax.optimization_barrier((line, packed))
    held = exchange(packed.reshape((2 * BANDS, CLASS) + block), ("row", "col"), SPREAD)
    held = held.reshape(2, BANDS * CLASS * BS, BS)
    (line,) = call(choose_kernel, "choose", [((2,) + block, jnp.bfloat16)], (line,), cols)
    outs = [((BS, BANDS * CLASS * BS), jnp.bfloat16), ((2, 1, BS), jnp.float32), ((BANDS * CLASS,), jnp.int32)]
    left, weights, picks = call(pick_kernel, "pick", outs, lines(line), cols, 8, **lists)
    outs = [((Y,) + block, jnp.float32)]
    (sums,) = call(multiply_kernel, "multiply", outs, (left, held), cols, 16, cost_estimate=flops(128))

    outs = [(block, jnp.float32), ((2,) + block, jnp.bfloat16)]
    square, half = call(square_kernel, "square", outs, (exchange(sums, "col", Y_LINES),), cols)

    line = lines(half)
    scalars = (win_cols, picks)
    keep, send = call(partial_kernel, "partials", shares, (*line, held), scalars, 16, cost_estimate=flops(128))
    both = gather(send, Y_NEAR)
    cube = keep + weights[0] * both[0] + weights[1] * both[1]
    return (3.0 * square - 2.0 * cube).astype(jnp.bfloat16)[None, None]


def solution(mesh):
    return jax.shard_map(
        on_device,
        mesh=mesh,
        in_specs=(P("row", "col", None, None), P("row", "col", None, None, None, None), P()),
        out_specs=P("row", "col", None, None),
        check_vma=False,
    )
```

```python
import jax
import jax.numpy as jnp
from jax import lax
from jax.experimental import pallas as pl
from jax.experimental.pallas import tpu as pltpu
from jax.sharding import PartitionSpec as P

BS = 128
BANDS = 8
GROUP = 12
LIVE = 8
Z, Y, C = 12, 4, 2
N_COL = Z * Y * C
QUADS = 2 * Z

CLASS = LIVE // 2
STEP = 4


def col_of(z, y, c):
    return (z * Y + y) * C + c


Y_LINES = [[col_of(z, y, c) for y in range(Y)] for z in range(Z) for c in range(C)]
Y_NEAR = [[col_of(z, 2 * h + p, c) for p in range(2)] for z in range(Z) for h in range(2) for c in range(C)]
Z_LINES = [[col_of(z, y, (2 * z // Z + c) % C) for z in range(Z)] for y in range(Y) for c in range(C)]
SWAP = [(s, s ^ 1) for s in range(N_COL)]
SPREAD = [[row * N_COL + col for col in pair for row in range(BANDS)] for pair in Y_NEAR]


def place():
    col = lax.axis_index("col")
    return lax.axis_index("row"), col, lax.rem(col, C), lax.rem(col // C, 2)


def pair_alive(cols_ref, window, first):
    return [cols_ref[window, first + p * C] >= 0 for p in range(2)]


def member_of(alive, k):
    return jnp.where(alive[0] & alive[1], k, jnp.where(alive[0], 0, 1))


def list_live(cols_ref, list_ref, window, band, k, value):
    count, singles = jnp.int32(0), jnp.int32(0)
    for n in range(GROUP // 2):
        quad, core = divmod(n, C)
        alive = pair_alive(cols_ref, window, band * GROUP + quad * 4 + core)
        single = alive[0] != alive[1]
        taken = (alive[0] & alive[1]) | (single & (lax.rem(singles, 2) == k))
        list_ref[jnp.minimum(count, CLASS)] = value(quad, core, member_of(alive, k))
        count = count + taken.astype(jnp.int32)
        singles = singles + single.astype(jnp.int32)
    return count


def list_both(cols_ref, lists, window, band):
    counts, singles = [jnp.int32(0)] * 2, jnp.int32(0)
    for n in range(GROUP // 2):
        quad, core = divmod(n, C)
        slot = quad * 4 + core
        alive = [a.astype(jnp.int32) for a in pair_alive(cols_ref, window, band * GROUP + slot)]
        both, single = alive[0] & alive[1], alive[0] ^ alive[1]
        lists[0, jnp.minimum(counts[0], CLASS)] = slot + C * (1 - alive[0])
        lists[1, jnp.minimum(counts[1], CLASS)] = slot + C * alive[1]
        odd = singles & 1
        counts[0] = counts[0] + (both | (single & (1 - odd)))
        counts[1] = counts[1] + (both | (single & odd))
        singles = singles + single
    return counts


def pack_kernel(cols_ref, couple_ref, out_ref, lists):
    band = lax.axis_index("row")
    for i in range(STEP):
        slots = lists.at[i]
        counts = list_both(cols_ref, slots, pl.program_id(0) * STEP + i, band)
        for k in range(2):
            for j in range(CLASS):
                out_ref[k, i, j] = couple_ref[i, jnp.where(j < counts[k], slots[k, j], 0)]


def pack(win_cols, couple):
    return pl.pallas_call(
        pack_kernel,
        out_shape=jax.ShapeDtypeStruct((2, BANDS, CLASS, BS, BS), couple.dtype),
        grid=(BANDS // STEP,),
        in_specs=[
            pl.BlockSpec(memory_space=pltpu.SMEM),
            pl.BlockSpec((STEP, GROUP, BS, BS), lambda i: (i, 0, 0, 0)),
        ],
        out_specs=pl.BlockSpec((2, STEP, CLASS, BS, BS), lambda i: (0, i, 0, 0, 0)),
        scratch_shapes=[pltpu.SMEM((STEP, 2, CLASS + 1), jnp.int32)],
        cost_estimate=pl.CostEstimate(flops=0, bytes_accessed=5 << 20, transcendentals=0),
        compiler_params=pltpu.CompilerParams(vmem_limit_bytes=56 << 20),
        name="pack",
    )(win_cols, couple)


def copies_kernel(x_ref, out_ref):
    for y in range(Y):
        out_ref[y] = x_ref[0]


def choose_kernel(cols_ref, line_ref, out_ref):
    row, col, core, near = place()
    first = col // (Y * C) * (Y * C) + core
    for h in range(2):
        alive = pair_alive(cols_ref, row, first + 2 * h * C)
        out_ref[h] = line_ref[2 * h + member_of(alive, near)]


def list_picks(cols_ref, list_ref, picks_ref):
    row, col, core, near = place()
    line = lax.rem(col // (N_COL // 2) + core, 2)
    for band in range(BANDS):
        where = lambda quad, c, _, band=band: (
            band * 3 + quad + QUADS * lax.rem(line + c + 2 * (band * 3 + quad) // QUADS, 2)
        )
        count = list_live(cols_ref, list_ref, row, band, near, where)
        for j in range(CLASS):
            picks_ref[band * CLASS + j] = jnp.where(j < count, list_ref[j], -1)


def picked(picks_ref, own_ref, other_ref):
    blocks = []
    for n in range(BANDS * CLASS):
        pick = picks_ref[n]
        inside = lax.rem(jnp.maximum(pick, 0), QUADS)
        block = jnp.where(pick < QUADS, own_ref[inside], other_ref[inside])
        blocks.append(jnp.where(pick >= 0, block, jnp.zeros_like(block)))
    return jnp.concatenate(blocks, axis=1)


def multiply(cols_ref, left, m_ref):
    row, col, _, near = place()
    alive = pair_alive(cols_ref, row, col - near * C)
    chosen = [m_ref[member_of(alive, k)] for k in range(2)]
    product = jnp.dot(left, jnp.concatenate(chosen, axis=1), preferred_element_type=jnp.float32)
    return product[:, :BS], product[:, BS:]


def pick_kernel(cols_ref, own_ref, other_ref, left_ref, weights_ref, picks_ref, list_ref):
    near = place()[3]
    for p in range(2):
        weights_ref[p] = jnp.full((1, BS), (near != p).astype(jnp.float32))
    list_picks(cols_ref, list_ref, picks_ref)
    left_ref[...] = picked(picks_ref, own_ref, other_ref)


def multiply_kernel(cols_ref, left_ref, m_ref, out_ref):
    shares = multiply(cols_ref, left_ref[...], m_ref)
    for y in range(Y):
        out_ref[y] = shares[y % 2]


def partial_kernel(cols_ref, picks_ref, own_ref, other_ref, m_ref, keep_ref, send_ref):
    shares = multiply(cols_ref, picked(picks_ref, own_ref, other_ref), m_ref)
    row, col, _, near = place()
    keep = jnp.where(near == 0, *shares)
    send = jnp.where(near == 0, *shares[::-1])
    keep_ref[...] = jnp.where(cols_ref[row, col] >= 0, keep, 0.0)
    send_ref[0] = jnp.where(cols_ref[row, col ^ C] >= 0, send, 0.0)


def square_kernel(cols_ref, shares_ref, square_ref, half_ref):
    row, col, _, _ = place()
    h = lax.rem(col // (2 * C), 2)
    total = shares_ref[2 * h] + shares_ref[2 * h + 1]
    square_ref[...] = jnp.where(cols_ref[row, col] >= 0, total, 0.0)
    for pair in range(2):
        half_ref[pair] = (shares_ref[2 * pair] + shares_ref[2 * pair + 1]).astype(half_ref.dtype)


def call(kernel, name, outs, arrays, scalars=(), grant=4, **options):
    smem, vmem = (pl.BlockSpec(memory_space=space) for space in (pltpu.SMEM, pltpu.VMEM))
    return pl.pallas_call(
        kernel,
        out_shape=[jax.ShapeDtypeStruct(shape, dtype) for shape, dtype in outs],
        in_specs=[smem] * len(scalars) + [vmem] * len(arrays),
        out_specs=[smem if dtype == jnp.int32 else vmem for _, dtype in outs],
        compiler_params=pltpu.CompilerParams(vmem_limit_bytes=grant << 20),
        name=name,
        **options,
    )(*scalars, *arrays)


def gather(value, groups):
    return lax.all_gather(value, "col", axis=0, tiled=True, axis_index_groups=groups)


def exchange(value, axis, groups):
    return lax.all_to_all(value, axis, split_axis=0, concat_axis=0, tiled=True, axis_index_groups=groups)


def lines(line):
    own = gather(line, Z_LINES)
    return own, lax.ppermute(own, "col", SWAP)


def on_device(win_vals, couple_vals, win_cols):
    block, cols = (BS, BS), (win_cols,)
    lists = dict(scratch_shapes=[pltpu.SMEM((CLASS + 1,), jnp.int32)])
    flops = lambda count: pl.CostEstimate(flops=count * BS**3, bytes_accessed=4 << 20, transcendentals=0)
    shares = [(block, jnp.float32), ((1,) + block, jnp.float32)]

    packed = pack(win_cols, couple_vals[0, 0])
    (line,) = call(copies_kernel, "copies", [((Y,) + block, jnp.bfloat16)], (win_vals[0],))
    line = exchange(line, "col", Y_LINES)
    line, packed = lax.optimization_barrier((line, packed))
    held = exchange(packed.reshape((2 * BANDS, CLASS) + block), ("row", "col"), SPREAD)
    held = held.reshape(2, BANDS * CLASS * BS, BS)
    (line,) = call(choose_kernel, "choose", [((2,) + block, jnp.bfloat16)], (line,), cols)
    outs = [((BS, BANDS * CLASS * BS), jnp.bfloat16), ((2, 1, BS), jnp.float32), ((BANDS * CLASS,), jnp.int32)]
    left, weights, picks = call(pick_kernel, "pick", outs, lines(line), cols, 8, **lists)
    outs = [((Y,) + block, jnp.float32)]
    (sums,) = call(multiply_kernel, "multiply", outs, (left, held), cols, 16, cost_estimate=flops(128))

    outs = [(block, jnp.float32), ((2,) + block, jnp.bfloat16)]
    square, half = call(square_kernel, "square", outs, (exchange(sums, "col", Y_LINES),), cols)

    line = lines(half)
    scalars = (win_cols, picks)
    keep, send = call(partial_kernel, "partials", shares, (*line, held), scalars, 16, cost_estimate=flops(128))
    both = gather(send, Y_NEAR)
    cube = keep + weights[0] * both[0] + weights[1] * both[1]
    return (3.0 * square - 2.0 * cube).astype(jnp.bfloat16)[None, None]


def solution(mesh):
    return jax.shard_map(
        on_device,
        mesh=mesh,
        in_specs=(P("row", "col", None, None), P("row", "col", None, None, None, None), P()),
        out_specs=P("row", "col", None, None),
        check_vma=False,
    )
```

```python
import jax
import jax.numpy as jnp
from jax import lax
from jax.experimental import pallas as pl
from jax.experimental.pallas import tpu as pltpu
from jax.sharding import PartitionSpec as P

BS = 128
BANDS = 8
GROUP = 12
LIVE = 8
Z, Y, C = 12, 4, 2
N_COL = Z * Y * C
QUADS = 2 * Z

CLASS = LIVE // 2
STEP = 4


def col_of(z, y, c):
    return (z * Y + y) * C + c


Y_LINES = [[col_of(z, y, c) for y in range(Y)] for z in range(Z) for c in range(C)]
Y_NEAR = [[col_of(z, 2 * h + p, c) for p in range(2)] for z in range(Z) for h in range(2) for c in range(C)]
TURN = 7
Z_LINES = [[col_of(z, y, (z // TURN + c) % C) for z in range(Z)] for y in range(Y) for c in range(C)]
SWAP = [(s, s ^ 1) for s in range(N_COL)]
SPREAD = [[row * N_COL + col for col in pair for row in range(BANDS)] for pair in Y_NEAR]


def place():
    col = lax.axis_index("col")
    return lax.axis_index("row"), col, lax.rem(col, C), lax.rem(col // C, 2)


def pair_alive(cols_ref, window, first):
    return [cols_ref[window, first + p * C] >= 0 for p in range(2)]


def member_of(alive, k):
    return jnp.where(alive[0] & alive[1], k, jnp.where(alive[0], 0, 1))


def list_live(cols_ref, list_ref, window, band, k, value):
    count, singles = jnp.int32(0), jnp.int32(0)
    for n in range(GROUP // 2):
        quad, core = divmod(n, C)
        alive = pair_alive(cols_ref, window, band * GROUP + quad * 4 + core)
        single = alive[0] != alive[1]
        taken = (alive[0] & alive[1]) | (single & (lax.rem(singles, 2) == k))
        list_ref[jnp.minimum(count, CLASS)] = value(quad, core, member_of(alive, k))
        count = count + taken.astype(jnp.int32)
        singles = singles + single.astype(jnp.int32)
    return count


def list_both(cols_ref, lists, window, band):
    counts, singles = [jnp.int32(0)] * 2, jnp.int32(0)
    for n in range(GROUP // 2):
        quad, core = divmod(n, C)
        slot = quad * 4 + core
        alive = [a.astype(jnp.int32) for a in pair_alive(cols_ref, window, band * GROUP + slot)]
        both, single = alive[0] & alive[1], alive[0] ^ alive[1]
        lists[0, jnp.minimum(counts[0], CLASS)] = slot + C * (1 - alive[0])
        lists[1, jnp.minimum(counts[1], CLASS)] = slot + C * alive[1]
        odd = singles & 1
        counts[0] = counts[0] + (both | (single & (1 - odd)))
        counts[1] = counts[1] + (both | (single & odd))
        singles = singles + single
    return counts


def pack_kernel(cols_ref, couple_ref, out_ref, lists):
    band = lax.axis_index("row")
    for i in range(STEP):
        slots = lists.at[i]
        counts = list_both(cols_ref, slots, pl.program_id(0) * STEP + i, band)
        for k in range(2):
            for j in range(CLASS):
                out_ref[k, i, j] = couple_ref[i, jnp.where(j < counts[k], slots[k, j], 0)]


def pack(win_cols, couple):
    return pl.pallas_call(
        pack_kernel,
        out_shape=jax.ShapeDtypeStruct((2, BANDS, CLASS, BS, BS), couple.dtype),
        grid=(BANDS // STEP,),
        in_specs=[
            pl.BlockSpec(memory_space=pltpu.SMEM),
            pl.BlockSpec((STEP, GROUP, BS, BS), lambda i: (i, 0, 0, 0)),
        ],
        out_specs=pl.BlockSpec((2, STEP, CLASS, BS, BS), lambda i: (0, i, 0, 0, 0)),
        scratch_shapes=[pltpu.SMEM((STEP, 2, CLASS + 1), jnp.int32)],
        cost_estimate=pl.CostEstimate(flops=0, bytes_accessed=5 << 20, transcendentals=0),
        compiler_params=pltpu.CompilerParams(vmem_limit_bytes=56 << 20),
        name="pack",
    )(win_cols, couple)


def copies_kernel(x_ref, out_ref):
    for y in range(Y):
        out_ref[y] = x_ref[0]


def choose_kernel(cols_ref, line_ref, out_ref):
    row, col, core, near = place()
    first = col // (Y * C) * (Y * C) + core
    for h in range(2):
        alive = pair_alive(cols_ref, row, first + 2 * h * C)
        out_ref[h] = line_ref[2 * h + member_of(alive, near)]


def list_picks(cols_ref, list_ref, picks_ref):
    row, col, core, near = place()
    line = lax.rem(col // (TURN * Y * C) + core, 2)
    for band in range(BANDS):
        where = lambda quad, c, _, band=band: (
            band * 3 + quad + QUADS * lax.rem(line + c + (band * 3 + quad) // (2 * TURN), 2)
        )
        count = list_live(cols_ref, list_ref, row, band, near, where)
        for j in range(CLASS):
            picks_ref[band * CLASS + j] = jnp.where(j < count, list_ref[j], -1)


def picked(picks_ref, own_ref, other_ref):
    blocks = []
    for n in range(BANDS * CLASS):
        pick = picks_ref[n]
        inside = lax.rem(jnp.maximum(pick, 0), QUADS)
        block = jnp.where(pick < QUADS, own_ref[inside], other_ref[inside])
        blocks.append(jnp.where(pick >= 0, block, jnp.zeros_like(block)))
    return jnp.concatenate(blocks, axis=1)


def multiply(cols_ref, left, m_ref):
    row, col, _, near = place()
    alive = pair_alive(cols_ref, row, col - near * C)
    chosen = [m_ref[member_of(alive, k)] for k in range(2)]
    product = jnp.dot(left, jnp.concatenate(chosen, axis=1), preferred_element_type=jnp.float32)
    return product[:, :BS], product[:, BS:]


def pick_kernel(cols_ref, own_ref, other_ref, left_ref, weights_ref, picks_ref, list_ref):
    near = place()[3]
    for p in range(2):
        weights_ref[p] = jnp.full((1, BS), (near != p).astype(jnp.float32))
    list_picks(cols_ref, list_ref, picks_ref)
    left_ref[...] = picked(picks_ref, own_ref, other_ref)


def multiply_kernel(cols_ref, left_ref, m_ref, out_ref):
    shares = multiply(cols_ref, left_ref[...], m_ref)
    for y in range(Y):
        out_ref[y] = shares[y % 2]


def partial_kernel(cols_ref, picks_ref, own_ref, other_ref, m_ref, keep_ref, send_ref):
    shares = multiply(cols_ref, picked(picks_ref, own_ref, other_ref), m_ref)
    row, col, _, near = place()
    keep = jnp.where(near == 0, *shares)
    send = jnp.where(near == 0, *shares[::-1])
    keep_ref[...] = jnp.where(cols_ref[row, col] >= 0, keep, 0.0)
    send_ref[0] = jnp.where(cols_ref[row, col ^ C] >= 0, send, 0.0)


def square_kernel(cols_ref, shares_ref, square_ref, half_ref):
    row, col, _, _ = place()
    h = lax.rem(col // (2 * C), 2)
    total = shares_ref[2 * h] + shares_ref[2 * h + 1]
    square_ref[...] = jnp.where(cols_ref[row, col] >= 0, total, 0.0)
    for pair in range(2):
        half_ref[pair] = (shares_ref[2 * pair] + shares_ref[2 * pair + 1]).astype(half_ref.dtype)


def call(kernel, name, outs, arrays, scalars=(), grant=4, **options):
    smem, vmem = (pl.BlockSpec(memory_space=space) for space in (pltpu.SMEM, pltpu.VMEM))
    return pl.pallas_call(
        kernel,
        out_shape=[jax.ShapeDtypeStruct(shape, dtype) for shape, dtype in outs],
        in_specs=[smem] * len(scalars) + [vmem] * len(arrays),
        out_specs=[smem if dtype == jnp.int32 else vmem for _, dtype in outs],
        compiler_params=pltpu.CompilerParams(vmem_limit_bytes=grant << 20),
        name=name,
        **options,
    )(*scalars, *arrays)


def gather(value, groups):
    return lax.all_gather(value, "col", axis=0, tiled=True, axis_index_groups=groups)


def exchange(value, axis, groups):
    return lax.all_to_all(value, axis, split_axis=0, concat_axis=0, tiled=True, axis_index_groups=groups)


def lines(line):
    own = gather(line, Z_LINES)
    return own, lax.ppermute(own, "col", SWAP)


def on_device(win_vals, couple_vals, win_cols):
    block, cols = (BS, BS), (win_cols,)
    lists = dict(scratch_shapes=[pltpu.SMEM((CLASS + 1,), jnp.int32)])
    flops = lambda count: pl.CostEstimate(flops=count * BS**3, bytes_accessed=4 << 20, transcendentals=0)
    shares = [(block, jnp.float32), ((1,) + block, jnp.float32)]

    packed = pack(win_cols, couple_vals[0, 0])
    (line,) = call(copies_kernel, "copies", [((Y,) + block, jnp.bfloat16)], (win_vals[0],))
    line = exchange(line, "col", Y_LINES)
    line, packed = lax.optimization_barrier((line, packed))
    held = exchange(packed.reshape((2 * BANDS, CLASS) + block), ("row", "col"), SPREAD)
    held = held.reshape(2, BANDS * CLASS * BS, BS)
    (line,) = call(choose_kernel, "choose", [((2,) + block, jnp.bfloat16)], (line,), cols)
    outs = [((BS, BANDS * CLASS * BS), jnp.bfloat16), ((2, 1, BS), jnp.float32), ((BANDS * CLASS,), jnp.int32)]
    left, weights, picks = call(pick_kernel, "pick", outs, lines(line), cols, 8, **lists)
    outs = [((Y,) + block, jnp.float32)]
    (sums,) = call(multiply_kernel, "multiply", outs, (left, held), cols, 16, cost_estimate=flops(128))

    outs = [(block, jnp.float32), ((2,) + block, jnp.bfloat16)]
    square, half = call(square_kernel, "square", outs, (exchange(sums, "col", Y_LINES),), cols)

    line = lines(half)
    scalars = (win_cols, picks)
    keep, send = call(partial_kernel, "partials", shares, (*line, held), scalars, 16, cost_estimate=flops(128))
    both = gather(send, Y_NEAR)
    cube = keep + weights[0] * both[0] + weights[1] * both[1]
    return (3.0 * square - 2.0 * cube).astype(jnp.bfloat16)[None, None]


def solution(mesh):
    return jax.shard_map(
        on_device,
        mesh=mesh,
        in_specs=(P("row", "col", None, None), P("row", "col", None, None, None, None), P()),
        out_specs=P("row", "col", None, None),
        check_vma=False,
    )
```

```python
import jax
import jax.numpy as jnp
from jax import lax
from jax.experimental import pallas as pl
from jax.experimental.pallas import tpu as pltpu
from jax.sharding import PartitionSpec as P

BS = 128
BANDS = 8
GROUP = 12
LIVE = 8
Z, Y, C = 12, 4, 2
N_COL = Z * Y * C
QUADS = 2 * Z

CLASS = LIVE // 2
STEP = 4


def col_of(z, y, c):
    return (z * Y + y) * C + c


Y_LINES = [[col_of(z, y, c) for y in range(Y)] for z in range(Z) for c in range(C)]
Y_NEAR = [[col_of(z, 2 * h + p, c) for p in range(2)] for z in range(Z) for h in range(2) for c in range(C)]
Z_LINES = [[col_of(z, y, (2 * z // Z + c) % C) for z in range(Z)] for y in range(Y) for c in range(C)]
SWAP = [(s, s ^ 1) for s in range(N_COL)]
SPREAD = [[row * N_COL + col for col in pair for row in range(BANDS)] for pair in Y_NEAR]


def place():
    col = lax.axis_index("col")
    return lax.axis_index("row"), col, lax.rem(col, C), lax.rem(col // C, 2)


def pair_alive(cols_ref, window, first):
    return [cols_ref[window, first + p * C] >= 0 for p in range(2)]


def member_of(alive, k):
    return jnp.where(alive[0] & alive[1], k, jnp.where(alive[0], 0, 1))


def list_live(cols_ref, list_ref, window, band, k, value):
    count, singles = jnp.int32(0), jnp.int32(0)
    for n in range(GROUP // 2):
        quad, core = divmod(n, C)
        alive = pair_alive(cols_ref, window, band * GROUP + quad * 4 + core)
        single = alive[0] != alive[1]
        taken = (alive[0] & alive[1]) | (single & (lax.rem(singles, 2) == k))
        list_ref[jnp.minimum(count, CLASS)] = value(quad, core, member_of(alive, k))
        count = count + taken.astype(jnp.int32)
        singles = singles + single.astype(jnp.int32)
    return count


def list_both(cols_ref, lists, window, band):
    counts, singles = [jnp.int32(0)] * 2, jnp.int32(0)
    for n in range(GROUP // 2):
        quad, core = divmod(n, C)
        slot = quad * 4 + core
        alive = [a.astype(jnp.int32) for a in pair_alive(cols_ref, window, band * GROUP + slot)]
        both, single = alive[0] & alive[1], alive[0] ^ alive[1]
        lists[0, jnp.minimum(counts[0], CLASS)] = slot + C * (1 - alive[0])
        lists[1, jnp.minimum(counts[1], CLASS)] = slot + C * alive[1]
        odd = singles & 1
        counts[0] = counts[0] + (both | (single & (1 - odd)))
        counts[1] = counts[1] + (both | (single & odd))
        singles = singles + single
    return counts


def pack_kernel(cols_ref, couple_ref, out_ref, lists):
    band = lax.axis_index("row")
    for i in range(STEP):
        slots = lists.at[i]
        counts = list_both(cols_ref, slots, pl.program_id(0) * STEP + i, band)
        for k in range(2):
            for j in range(CLASS):
                out_ref[k, i, j] = couple_ref[i, jnp.where(j < counts[k], slots[k, j], 0)]


def pack(win_cols, couple):
    return pl.pallas_call(
        pack_kernel,
        out_shape=jax.ShapeDtypeStruct((2, BANDS, CLASS, BS, BS), couple.dtype),
        grid=(BANDS // STEP,),
        in_specs=[
            pl.BlockSpec(memory_space=pltpu.SMEM),
            pl.BlockSpec((STEP, GROUP, BS, BS), lambda i: (i, 0, 0, 0)),
        ],
        out_specs=pl.BlockSpec((2, STEP, CLASS, BS, BS), lambda i: (0, i, 0, 0, 0)),
        scratch_shapes=[pltpu.SMEM((STEP, 2, CLASS + 1), jnp.int32)],
        cost_estimate=pl.CostEstimate(flops=0, bytes_accessed=5 << 20, transcendentals=0),
        compiler_params=pltpu.CompilerParams(vmem_limit_bytes=56 << 20),
        name="pack",
    )(win_cols, couple)


def copies_kernel(x_ref, out_ref):
    for y in range(Y):
        out_ref[y] = x_ref[0]


def choose_kernel(cols_ref, line_ref, out_ref):
    row, col, core, near = place()
    first = col // (Y * C) * (Y * C) + core
    for h in range(2):
        alive = pair_alive(cols_ref, row, first + 2 * h * C)
        out_ref[h] = line_ref[2 * h + member_of(alive, near)]


def list_picks(cols_ref, list_ref, picks_ref):
    row, col, core, near = place()
    line = lax.rem(col // (N_COL // 2) + core, 2)
    for band in range(BANDS):
        where = lambda quad, c, _, band=band: (
            band * 3 + quad + QUADS * lax.rem(line + c + 2 * (band * 3 + quad) // QUADS, 2)
        )
        count = list_live(cols_ref, list_ref, row, band, near, where)
        for j in range(CLASS):
            picks_ref[band * CLASS + j] = jnp.where(j < count, list_ref[j], -1)


def picked(picks_ref, own_ref, other_ref):
    blocks = []
    for n in range(BANDS * CLASS):
        pick = picks_ref[n]
        inside = lax.rem(jnp.maximum(pick, 0), QUADS)
        block = jnp.where(pick < QUADS, own_ref[inside], other_ref[inside])
        blocks.append(jnp.where(pick >= 0, block, jnp.zeros_like(block)))
    return jnp.concatenate(blocks, axis=1)


def multiply(cols_ref, left, m_ref):
    row, col, _, near = place()
    alive = pair_alive(cols_ref, row, col - near * C)
    chosen = [m_ref[member_of(alive, k)] for k in range(2)]
    product = jnp.dot(left, jnp.concatenate(chosen, axis=1), preferred_element_type=jnp.float32)
    return product[:, :BS], product[:, BS:]


def pick_kernel(cols_ref, own_ref, other_ref, left_ref, weights_ref, picks_ref, list_ref):
    near = place()[3]
    for p in range(2):
        weights_ref[p] = jnp.full((1, BS), (near != p).astype(jnp.float32))
    list_picks(cols_ref, list_ref, picks_ref)
    left_ref[...] = picked(picks_ref, own_ref, other_ref)


def multiply_kernel(cols_ref, left_ref, m_ref, out_ref):
    shares = multiply(cols_ref, left_ref[...], m_ref)
    for y in range(Y):
        out_ref[y] = shares[y % 2]


def partial_kernel(cols_ref, picks_ref, own_ref, other_ref, m_ref, keep_ref, send_ref):
    shares = multiply(cols_ref, picked(picks_ref, own_ref, other_ref), m_ref)
    row, col, _, near = place()
    keep = jnp.where(near == 0, *shares)
    send = jnp.where(near == 0, *shares[::-1])
    keep_ref[...] = jnp.where(cols_ref[row, col] >= 0, keep, 0.0)
    send_ref[0] = jnp.where(cols_ref[row, col ^ C] >= 0, send, 0.0)


def square_kernel(cols_ref, shares_ref, square_ref, half_ref):
    row, col, _, _ = place()
    h = lax.rem(col // (2 * C), 2)
    total = shares_ref[2 * h] + shares_ref[2 * h + 1]
    square_ref[...] = jnp.where(cols_ref[row, col] >= 0, total, 0.0)
    for pair in range(2):
        half_ref[pair] = (shares_ref[2 * pair] + shares_ref[2 * pair + 1]).astype(half_ref.dtype)


def call(kernel, name, outs, arrays, scalars=(), grant=4, **options):
    smem, vmem = (pl.BlockSpec(memory_space=space) for space in (pltpu.SMEM, pltpu.VMEM))
    return pl.pallas_call(
        kernel,
        out_shape=[jax.ShapeDtypeStruct(shape, dtype) for shape, dtype in outs],
        in_specs=[smem] * len(scalars) + [vmem] * len(arrays),
        out_specs=[smem if dtype == jnp.int32 else vmem for _, dtype in outs],
        compiler_params=pltpu.CompilerParams(vmem_limit_bytes=grant << 20),
        name=name,
        **options,
    )(*scalars, *arrays)


def gather(value, groups):
    return lax.all_gather(value, "col", axis=0, tiled=True, axis_index_groups=groups)


def exchange(value, axis, groups):
    return lax.all_to_all(value, axis, split_axis=0, concat_axis=0, tiled=True, axis_index_groups=groups)


def lines(line):
    own = gather(line, Z_LINES)
    return own, lax.ppermute(own, "col", SWAP)


def on_device(win_vals, couple_vals, win_cols):
    block, cols = (BS, BS), (win_cols,)
    lists = dict(scratch_shapes=[pltpu.SMEM((CLASS + 1,), jnp.int32)])
    flops = lambda count: pl.CostEstimate(flops=count * BS**3, bytes_accessed=4 << 20, transcendentals=0)
    shares = [(block, jnp.float32), ((1,) + block, jnp.float32)]

    packed = pack(win_cols, couple_vals[0, 0])
    line = jnp.broadcast_to(win_vals[0], (Y,) + block)
    line = exchange(line, "col", Y_LINES)
    line, packed = lax.optimization_barrier((line, packed))
    held = exchange(packed.reshape((2 * BANDS, CLASS) + block), ("row", "col"), SPREAD)
    held = held.reshape(2, BANDS * CLASS * BS, BS)
    (line,) = call(choose_kernel, "choose", [((2,) + block, jnp.bfloat16)], (line,), cols)
    outs = [((BS, BANDS * CLASS * BS), jnp.bfloat16), ((2, 1, BS), jnp.float32), ((BANDS * CLASS,), jnp.int32)]
    left, weights, picks = call(pick_kernel, "pick", outs, lines(line), cols, 8, **lists)
    outs = [((Y,) + block, jnp.float32)]
    (sums,) = call(multiply_kernel, "multiply", outs, (left, held), cols, 16, cost_estimate=flops(128))

    outs = [(block, jnp.float32), ((2,) + block, jnp.bfloat16)]
    square, half = call(square_kernel, "square", outs, (exchange(sums, "col", Y_LINES),), cols)

    line = lines(half)
    scalars = (win_cols, picks)
    keep, send = call(partial_kernel, "partials", shares, (*line, held), scalars, 16, cost_estimate=flops(128))
    both = gather(send, Y_NEAR)
    cube = keep + weights[0] * both[0] + weights[1] * both[1]
    return (3.0 * square - 2.0 * cube).astype(jnp.bfloat16)[None, None]


def solution(mesh):
    return jax.shard_map(
        on_device,
        mesh=mesh,
        in_specs=(P("row", "col", None, None), P("row", "col", None, None, None, None), P()),
        out_specs=P("row", "col", None, None),
        check_vma=False,
    )
```
